512 devices in a mesh: gen: 16 (over z), train: 32 (over x, y, core).
Axes of the slice: x: 4, y: 4, z: 16, core: 2. Of those that a mesh axis runs over, the one named last changes fastest.
Arguments:
- gen_embed: float32 [16384, 256], P(('gen', 'train')), may hold values from -20 to 20, as said below
- train_embed: float32 [16384, 256], P(('train', 'gen')), may hold values from -20 to 20, as said below
- row_mass: float32 [16384], P('gen'), may hold values from 1 to 100, as said below
- col_mass: float32 [16384], P('train'), may hold values from 1 to 100, as said below
Outputs:
- row_potential: float32 [16384], P('gen')
- col_potential: float32 [16384], P('train')
- transport_cost: float32 [], replicated
The draws below stay inside these ranges and needn't reach their ends.
Inputs may be any that keep to these rules, and one draw needn't show every extreme that they name: `gen_embed`: finite embeddings. `train_embed`: finite embeddings. `row_mass`: positive masses. `col_mass`: positive masses.
All inputs are finite; a program needn't handle non-finite values.
Results may differ from the reference program's by a relative error of at most 0.0003.
Values sent between devices are 32-bit elements; how exact they have to be, the bound alone decides.
No kernel may reach another device: no remote copies, remote signals or barrier semaphores. Data moves between devices by JAX's collectives and lax.ppermute only.
A program may use at most 64 MiB of HBM per device.

```python
import jax
import jax.numpy as jnp
from jax import lax

D = 256
ROWS_G = 1024
ITERS = 3
N = 16384
M = 16384
N_GEN = 16


def embed_pair(key, spread, aligned):
    key_gen, key_train, key_gscale, key_tscale, key_near = jax.random.split(key, 5)
    gen_scale = jnp.exp(jax.random.uniform(key_gscale, (N, 1), jnp.float32) * jnp.log(spread))
    train_scale = jnp.exp(jax.random.uniform(key_tscale, (M, 1), jnp.float32) * jnp.log(spread))
    gen_rows = jax.random.normal(key_gen, (N, D), jnp.float32) * gen_scale
    train_rows = jax.random.normal(key_train, (M, D), jnp.float32) * train_scale
    nearby = train_rows[:aligned] + 0.3 * jax.random.normal(key_near, (aligned, D), jnp.float32)
    train_rows = train_rows.at[aligned:2 * aligned].set(nearby)
    gen_rows = gen_rows.at[:aligned].set(train_rows[:aligned])
    return (jnp.clip(gen_rows, -20.0, 20.0), jnp.clip(train_rows, -20.0, 20.0))


def draw_gen_embed(key, part):
    pair = embed_pair(key, 1.4, 0)
    return pair[0]


def draw_train_embed(key, part):
    pair = embed_pair(key, 1.4, 0)
    return pair[1]


def ramp_mass(key, count, slope):
    position = jnp.arange(count, dtype=jnp.float32) / (count - 1)
    factor = jnp.exp(jax.random.uniform(key, (count,), jnp.float32) * jnp.log(10.0))
    return (1.0 + slope * position) * factor


def draw_row_mass(key, part):
    key = jax.random.fold_in(key, 11)
    return ramp_mass(key, N, 2.0)


def draw_col_mass(key, part):
    key = jax.random.fold_in(key, 23)
    return ramp_mass(key, M, 2.0)


def setup_inputs(seed: int = 0) -> dict:
    keys = jax.random.split(jax.random.key(seed), 5)
    gen_embed = draw_gen_embed(jax.random.fold_in(keys[4], 71), 0)
    train_embed = draw_train_embed(jax.random.fold_in(keys[4], 71), 0)
    row_mass = draw_row_mass(jax.random.fold_in(keys[4], 71), 0)
    col_mass = draw_col_mass(jax.random.fold_in(keys[4], 71), 0)
    return dict(gen_embed=gen_embed, train_embed=train_embed, row_mass=row_mass, col_mass=col_mass)


EPSILON = 0.05


def block_costs(left_rows, right_rows):
    left_sq = jnp.sum(left_rows * left_rows, axis=1)
    right_sq = jnp.sum(right_rows * right_rows, axis=1)
    inner = jnp.dot(left_rows, right_rows.T, precision=lax.Precision.HIGHEST, preferred_element_type=jnp.float32)
    return (left_sq[:, None] + right_sq[None, :] - 2.0 * inner) / left_rows.shape[1]


def reference(gen_embed, train_embed, row_mass, col_mass):
    log_gen = jnp.log(row_mass) - jnp.log(jnp.sum(row_mass))
    log_train = jnp.log(col_mass) - jnp.log(jnp.sum(col_mass))
    gen_blocks = gen_embed.reshape(N_GEN, ROWS_G, D)
    log_gen_blocks = log_gen.reshape(N_GEN, ROWS_G)
    col_pot = jnp.zeros((M,), jnp.float32)
    row_pot = jnp.zeros((N,), jnp.float32)
    for iteration in range(ITERS):
        def row_update(block, col_now=col_pot):
            costs = block_costs(block, train_embed)
            scores = (col_now[None, :] - costs) / EPSILON + log_train[None, :]
            highest = jnp.max(scores, axis=1)
            totals = jnp.sum(jnp.exp(scores - highest[:, None]), axis=1)
            return -EPSILON * (highest + jnp.log(totals))

        row_pot = lax.map(row_update, gen_blocks).reshape(N)
        row_blocks = row_pot.reshape(N_GEN, ROWS_G)

        def col_step(carry, inputs):
            block, potent, log_weight = inputs
            costs = block_costs(block, train_embed)
            scores = (potent[:, None] - costs) / EPSILON + log_weight[:, None]
            running_max, running_sum = carry
            highest = jnp.maximum(running_max, jnp.max(scores, axis=0))
            new_sum = running_sum * jnp.exp(running_max - highest) + jnp.sum(jnp.exp(scores - highest[None, :]), axis=0)
            return (highest, new_sum), None

        start_carry = (jnp.full((M,), -jnp.inf, jnp.float32), jnp.zeros((M,), jnp.float32))
        (highest, totals), unused = lax.scan(col_step, start_carry, (gen_blocks, row_blocks, log_gen_blocks))
        col_pot = -EPSILON * (highest + jnp.log(totals))

    row_blocks = row_pot.reshape(N_GEN, ROWS_G)

    def cost_step(carry, inputs):
        block, potent, log_weight = inputs
        costs = block_costs(block, train_embed)
        log_plan = (potent[:, None] + col_pot[None, :] - costs) / EPSILON + log_weight[:, None] + log_train[None, :]
        return carry + jnp.sum(jnp.exp(log_plan) * costs), None

    transport, unused = lax.scan(cost_step, jnp.zeros((), jnp.float32), (gen_blocks, row_blocks, log_gen_blocks))
    return row_pot, col_pot, transport
```

```python
import jax
import jax.numpy as jnp
from jax import lax
from jax.sharding import PartitionSpec as P

ITERS = 3


EPSILON = 0.05


def exchange(values, axis, count):
    copies = jnp.broadcast_to(values[None], (count,) + values.shape)
    return lax.all_to_all(copies, axis, 0, 0)


def combine(logs):
    highest = jnp.max(logs, axis=0)
    return highest + jnp.log(jnp.sum(jnp.exp(logs - highest[None]), axis=0))


def shards(n_gen, n_train, gen_embed, train_embed, row_mass, col_mass):
    width = gen_embed.shape[1]
    rows, cols = row_mass.shape[0], col_mass.shape[0]
    gen_block = exchange(gen_embed, "train", n_train).reshape(rows, width)
    train_block = exchange(train_embed, "gen", n_gen).reshape(cols, width)
    gen_sq = jnp.sum(gen_block * gen_block, axis=1)
    train_sq = jnp.sum(train_block * train_block, axis=1)
    inner = jnp.dot(
        gen_block, train_block.T, precision=lax.Precision.HIGHEST, preferred_element_type=jnp.float32
    )
    affinity = (2.0 * inner - gen_sq[:, None] - train_sq[None, :]) * (1.0 / (width * EPSILON))

    log_gen = jnp.log(row_mass)
    log_train = jnp.log(col_mass)
    gen_local = jnp.broadcast_to(jnp.sum(row_mass), (128,))
    train_local = jnp.broadcast_to(jnp.sum(col_mass), (128,))
    col_pot = jnp.zeros((cols,), jnp.float32)
    log_gen_total = log_train_total = train_total = None
    for iteration in range(ITERS):
        scores = affinity + (col_pot + log_train)[None, :]
        highest = jnp.max(scores, axis=1)
        local = highest + jnp.log(jnp.sum(jnp.exp(scores - highest[:, None]), axis=1))
        if iteration == 0:
            got = exchange(jnp.concatenate([local, train_local]), "train", n_train)
            train_total = jnp.sum(got[:, rows])
            log_train_total = jnp.log(train_total)
            got = got[:, :rows]
        else:
            got = exchange(local, "train", n_train)
        row_pot = log_train_total - combine(got)
        scores = affinity + (row_pot + log_gen)[:, None]
        highest = jnp.max(scores, axis=0)
        weights = jnp.exp(scores - highest[None, :])
        total = jnp.sum(weights, axis=0)
        local = highest + jnp.log(total)
        if iteration == 0:
            got = exchange(jnp.concatenate([local, gen_local]), "gen", n_gen)
            log_gen_total = jnp.log(jnp.sum(got[:, cols]))
            got = got[:, :cols]
        elif iteration < ITERS - 1:
            got = exchange(local, "gen", n_gen)
        else:
            mean = jnp.sum(weights * affinity, axis=0) / total
            both = exchange(jnp.stack([local, mean]), "gen", n_gen)
            got = both[:, 0]
            share = jnp.exp(got - jnp.max(got, axis=0)[None])
            mean = jnp.sum(share * both[:, 1], axis=0) / jnp.sum(share, axis=0)
        col_pot = log_gen_total - combine(got)
    local_cost = -EPSILON * jnp.sum(col_mass * mean) / train_total
    transport = jnp.sum(exchange(jnp.broadcast_to(local_cost, (128,)), "train", n_train)[:, 0])
    return (EPSILON * row_pot, EPSILON * col_pot, transport)


def solution(mesh):
    in_specs = (P(("gen", "train"), None), P(("train", "gen"), None), P("gen"), P("train"))
    out_specs = (P("gen"), P("train"), P())

    def body(*args):
        return shards(mesh.shape["gen"], mesh.shape["train"], *args)

    return jax.shard_map(body, mesh=mesh, in_specs=in_specs, out_specs=out_specs, check_vma=False)
```

```python
import jax
import jax.numpy as jnp
from jax import lax
from jax.sharding import PartitionSpec as P

ITERS = 3


EPSILON = 0.05


def exchange(values, axis, count):
    copies = jnp.broadcast_to(values[None], (count,) + values.shape)
    return lax.all_to_all(copies, axis, 0, 0)


def combine(logs):
    highest = jnp.max(logs, axis=0)
    return highest + jnp.log(jnp.sum(jnp.exp(logs - highest[None]), axis=0))


def shards(n_gen, n_train, gen_embed, train_embed, row_mass, col_mass):
    width = gen_embed.shape[1]
    rows, cols = row_mass.shape[0], col_mass.shape[0]
    gen_block = exchange(gen_embed, "train", n_train).reshape(rows, width)
    train_block = lax.all_gather(train_embed, "gen", axis=0, tiled=True)
    gen_sq = jnp.sum(gen_block * gen_block, axis=1)
    train_sq = jnp.sum(train_block * train_block, axis=1)
    inner = jnp.dot(
        gen_block, train_block.T, precision=lax.Precision.HIGHEST, preferred_element_type=jnp.float32
    )
    affinity = (2.0 * inner - gen_sq[:, None] - train_sq[None, :]) * (1.0 / (width * EPSILON))

    log_gen = jnp.log(row_mass)
    log_train = jnp.log(col_mass)
    col_pot = jnp.zeros((cols,), jnp.float32)
    for iteration in range(ITERS):
        scores = affinity + (col_pot + log_train)[None, :]
        highest = jnp.max(scores, axis=1)
        local = highest + jnp.log(jnp.sum(jnp.exp(scores - highest[:, None]), axis=1))
        row_pot = -combine(exchange(local, "train", n_train))
        scores = affinity + (row_pot + log_gen)[:, None]
        highest = jnp.max(scores, axis=0)
        weights = jnp.exp(scores - highest[None, :])
        total = jnp.sum(weights, axis=0)
        local = highest + jnp.log(total)
        if iteration < ITERS - 1:
            col_pot = -combine(exchange(local, "gen", n_gen))
    mean = jnp.sum(weights * affinity, axis=0) / total
    mass = jnp.sum(row_mass.reshape(-1, cols), axis=0)
    got = exchange(jnp.stack([local, mean, mass]), "gen", n_gen)
    logs = got[:, 0]
    highest = jnp.max(logs, axis=0)
    share = jnp.exp(logs - highest[None])
    total = jnp.sum(share, axis=0)
    col_pot = -(highest + jnp.log(total))
    mean = jnp.sum(share * got[:, 1], axis=0) / total
    log_gen_total = jnp.log(jnp.sum(got[:, 2]))
    costs = jnp.sum((col_mass * mean).reshape(-1, 128), axis=0)
    mass = jnp.sum(col_mass.reshape(-1, 128), axis=0)
    got = exchange(jnp.stack([costs, mass]), "train", n_train)
    train_total = jnp.sum(got[:, 1])
    log_train_total = jnp.log(train_total)
    transport = -EPSILON * jnp.sum(got[:, 0]) / train_total
    row_shift = ITERS * log_train_total - (ITERS - 1) * log_gen_total
    col_shift = ITERS * (log_gen_total - log_train_total)
    return (EPSILON * (row_pot + row_shift), EPSILON * (col_pot + col_shift), transport)


def solution(mesh):
    in_specs = (P(("gen", "train"), None), P(("train", "gen"), None), P("gen"), P("train"))
    out_specs = (P("gen"), P("train"), P())

    def body(*args):
        return shards(mesh.shape["gen"], mesh.shape["train"], *args)

    return jax.shard_map(body, mesh=mesh, in_specs=in_specs, out_specs=out_specs, check_vma=False)
```

```python
import functools

import jax
import jax.numpy as jnp
from jax import lax
from jax.experimental import pallas as pl
from jax.experimental.pallas import tpu as pltpu
from jax.sharding import PartitionSpec as P

ITERS = 3


EPSILON = 0.05
LANES = 128
VMEM = pl.BlockSpec(memory_space=pltpu.VMEM)


def shape(*dims):
    return jax.ShapeDtypeStruct(dims, jnp.float32)


def call(kernel, outs, ins, scratch=(), in_specs=None, out_specs=None, limit=8 << 20):
    return pl.pallas_call(
        kernel,
        out_shape=outs,
        in_specs=in_specs or [VMEM] * len(ins),
        out_specs=out_specs or [VMEM] * len(outs),
        scratch_shapes=scratch,
        compiler_params=pltpu.CompilerParams(vmem_limit_bytes=limit),
    )(*ins)


def copies_kernel(values, out, sems):
    count = out.shape[0]
    moves = [pltpu.make_async_copy(values, out.at[k], sems.at[k]) for k in range(count)]
    for move in moves:
        move.start()
    for move in moves:
        move.wait()


def affinity_kernel(scale, gen, train, train_sq, out):
    step = 256
    for start in range(0, gen.shape[0], step):
        part = gen[start : start + step, :]
        inner = lax.dot_general(
            part,
            train[...],
            (((1,), (1,)), ((), ())),
            precision=lax.Precision.HIGHEST,
            preferred_element_type=jnp.float32,
        )
        part_sq = jnp.sum(part * part, axis=1, keepdims=True)
        out[start : start + step, :] = (2.0 * inner - part_sq - train_sq[...]) * scale


def pack_kernel(local, mean, mass, out):
    cols = local.shape[1]
    total = jnp.sum(mass[...], axis=0, keepdims=True)
    for k in range(out.shape[0]):
        out[k, :, 0:cols] = local[...]
        out[k, :, cols : 2 * cols] = mean[...]
        out[k, :, 2 * cols :] = total


def column_kernel(got, mass, col_pot, gen_mass, out):
    count, cols = got.shape[0], mass.shape[1]
    logs = [got[k, :, 0:cols] for k in range(count)]
    highest = functools.reduce(jnp.maximum, logs)
    total = weighted = jnp.zeros_like(highest)
    sums = jnp.zeros_like(gen_mass)
    for k in range(count):
        share = jnp.exp(logs[k] - highest)
        total += share
        weighted += share * got[k, :, cols : 2 * cols]
        sums += got[k, :, 2 * cols :]
    col_pot[...] = -(highest + jnp.log(total))
    gen_mass[...] = sums
    costs = mass[...] * (weighted / total)
    lanes = [slice(at, at + LANES) for at in range(0, cols, LANES)]
    cost = sum(costs[:, at] for at in lanes)
    train_mass = sum(mass[:, at] for at in lanes)
    for k in range(out.shape[0]):
        out[k, :, 0:LANES] = cost
        out[k, :, LANES:] = train_mass


def outputs_kernel(got, row_pot, col_pot, gen_mass, row_out, col_out, cost_out):
    sums = got[0]
    for k in range(1, got.shape[0]):
        sums += got[k]
    cost = jnp.sum(sums[:, 0:LANES], axis=1, keepdims=True)
    train_total = jnp.sum(sums[:, LANES:], axis=1, keepdims=True)
    log_train = jnp.log(train_total)
    log_gen = jnp.log(jnp.sum(gen_mass[...], axis=1, keepdims=True))
    row_out[...] = EPSILON * (row_pot[...] + (ITERS * log_train - (ITERS - 1) * log_gen))
    col_out[...] = EPSILON * (col_pot[...] + ITERS * (log_gen - log_train))
    cost_out[...] = -EPSILON * cost / train_total


def exchange(values, axis, count):
    copies = jnp.broadcast_to(values[None], (count,) + values.shape)
    return lax.all_to_all(copies, axis, 0, 0)


def combine(logs):
    highest = jnp.max(logs, axis=0)
    return highest + jnp.log(jnp.sum(jnp.exp(logs - highest[None]), axis=0))


def shards(n_gen, n_train, gen_embed, train_embed, row_mass, col_mass):
    width = gen_embed.shape[1]
    rows, cols = row_mass.shape[0], col_mass.shape[0]
    (copies,) = call(
        copies_kernel,
        [shape(n_train, *gen_embed.shape)],
        [gen_embed],
        scratch=[pltpu.SemaphoreType.DMA((n_train,))],
        out_specs=[pl.BlockSpec(memory_space=pl.ANY)],
        limit=1 << 20,
    )
    gen_block = lax.all_to_all(copies, "train", 0, 0).reshape(rows, width)
    train_block = lax.all_gather(train_embed, "gen", axis=0, tiled=True)
    train_sq = jnp.sum(train_block * train_block, axis=1)
    (affinity,) = call(
        functools.partial(affinity_kernel, 1.0 / (width * EPSILON)),
        [shape(rows, cols)],
        [gen_block, train_block, train_sq[None]],
    )

    log_gen = jnp.log(row_mass)
    log_train = jnp.log(col_mass)
    col_pot = jnp.zeros((cols,), jnp.float32)
    for iteration in range(ITERS):
        scores = affinity + (col_pot + log_train)[None, :]
        highest = jnp.max(scores, axis=1)
        local = highest + jnp.log(jnp.sum(jnp.exp(scores - highest[:, None]), axis=1))
        row_pot = -combine(exchange(local, "train", n_train))
        scores = affinity + (row_pot + log_gen)[:, None]
        highest = jnp.max(scores, axis=0)
        weights = jnp.exp(scores - highest[None, :])
        total = jnp.sum(weights, axis=0)
        local = highest + jnp.log(total)
        if iteration < ITERS - 1:
            col_pot = -combine(exchange(local, "gen", n_gen))
    mean = jnp.sum(weights * affinity, axis=0) / total
    small = 1 << 20
    (packed,) = call(
        pack_kernel,
        [shape(n_gen, 1, 2 * cols + LANES)],
        [local[None], mean[None], row_mass.reshape(-1, LANES)],
        limit=small,
    )
    got = lax.all_to_all(packed, "gen", 0, 0)
    col_pot, gen_mass, packed = call(
        column_kernel,
        [shape(1, cols), shape(1, LANES), shape(n_train, 1, 2 * LANES)],
        [got, col_mass[None]],
        limit=small,
    )
    got = lax.all_to_all(packed, "train", 0, 0)
    row_out, col_out, cost = call(
        outputs_kernel,
        [shape(rows // LANES, LANES), shape(1, cols), shape(1, 1)],
        [got, row_pot.reshape(-1, LANES), col_pot, gen_mass],
        limit=small,
    )
    return (row_out.reshape(rows), col_out.reshape(cols), cost.reshape(()))


def solution(mesh):
    in_specs = (P(("gen", "train"), None), P(("train", "gen"), None), P("gen"), P("train"))
    out_specs = (P("gen"), P("train"), P())

    def body(*args):
        return shards(mesh.shape["gen"], mesh.shape["train"], *args)

    return jax.shard_map(body, mesh=mesh, in_specs=in_specs, out_specs=out_specs, check_vma=False)
```

```python
import functools

import jax
import jax.numpy as jnp
from jax import lax
from jax.experimental import pallas as pl
from jax.experimental.pallas import tpu as pltpu
from jax.sharding import PartitionSpec as P

ITERS = 3


EPSILON = 0.05
LANES = 128
VMEM = pl.BlockSpec(memory_space=pltpu.VMEM)


def shape(*dims):
    return jax.ShapeDtypeStruct(dims, jnp.float32)


def call(kernel, outs, ins, limit=8 << 20):
    return pl.pallas_call(
        kernel,
        out_shape=outs,
        in_specs=[VMEM] * len(ins),
        out_specs=[VMEM] * len(outs),
        compiler_params=pltpu.CompilerParams(vmem_limit_bytes=limit),
    )(*ins)


def affinity_kernel(scale, twice_gen, train, train_sq, out):
    step = 256
    for start in range(0, twice_gen.shape[0], step):
        part = twice_gen[start : start + step, :]
        twice_inner = lax.dot_general(
            part,
            train[...],
            (((1,), (1,)), ((), ())),
            precision=lax.Precision.HIGHEST,
            preferred_element_type=jnp.float32,
        )
        part_sq = 0.25 * jnp.sum(part * part, axis=1, keepdims=True)
        out[start : start + step, :] = (twice_inner - part_sq - train_sq[...]) * scale


def pack_kernel(local, mean, mass, out):
    cols = local.shape[1]
    total = jnp.sum(mass[...], axis=0, keepdims=True)
    for k in range(out.shape[0]):
        out[k, :, 0:cols] = local[...]
        out[k, :, cols : 2 * cols] = mean[...]
        out[k, :, 2 * cols :] = total


def column_kernel(got, mass, col_pot, gen_mass, out):
    count, cols = got.shape[0], mass.shape[1]
    logs = [got[k, :, 0:cols] for k in range(count)]
    highest = functools.reduce(jnp.maximum, logs)
    total = weighted = jnp.zeros_like(highest)
    sums = jnp.zeros_like(gen_mass)
    for k in range(count):
        share = jnp.exp(logs[k] - highest)
        total += share
        weighted += share * got[k, :, cols : 2 * cols]
        sums += got[k, :, 2 * cols :]
    col_pot[...] = -(highest + jnp.log(total))
    gen_mass[...] = sums
    costs = mass[...] * (weighted / total)
    lanes = [slice(at, at + LANES) for at in range(0, cols, LANES)]
    cost = sum(costs[:, at] for at in lanes)
    train_mass = sum(mass[:, at] for at in lanes)
    for k in range(out.shape[0]):
        out[k, :, 0:LANES] = cost
        out[k, :, LANES:] = train_mass


def outputs_kernel(got, row_pot, col_pot, gen_mass, row_out, col_out, cost_out):
    sums = got[0]
    for k in range(1, got.shape[0]):
        sums += got[k]
    cost = jnp.sum(sums[:, 0:LANES], axis=1, keepdims=True)
    train_total = jnp.sum(sums[:, LANES:], axis=1, keepdims=True)
    log_train = jnp.log(train_total)
    log_gen = jnp.log(jnp.sum(gen_mass[...], axis=1, keepdims=True))
    row_out[...] = EPSILON * (row_pot[...] + (ITERS * log_train - (ITERS - 1) * log_gen))
    col_out[...] = EPSILON * (col_pot[...] + ITERS * (log_gen - log_train))
    cost_out[...] = -EPSILON * cost / train_total


def exchange(values, axis, count):
    copies = jnp.broadcast_to(values[None], (count,) + values.shape)
    return lax.all_to_all(copies, axis, 0, 0)


def combine(logs):
    highest = jnp.max(logs, axis=0)
    return highest + jnp.log(jnp.sum(jnp.exp(logs - highest[None]), axis=0))


def shards(n_gen, n_train, gen_embed, train_embed, row_mass, col_mass):
    width = gen_embed.shape[1]
    rows, cols = row_mass.shape[0], col_mass.shape[0]
    gen_block = exchange(gen_embed, "train", n_train).reshape(rows, width)
    train_block = lax.all_gather(train_embed, "gen", axis=0, tiled=True)
    train_sq = jnp.sum(train_block * train_block, axis=1)
    (affinity,) = call(
        functools.partial(affinity_kernel, 1.0 / (width * EPSILON)),
        [shape(rows, cols)],
        [2.0 * gen_block, train_block, train_sq[None]],
    )

    log_gen = jnp.log(row_mass)
    log_train = jnp.log(col_mass)
    col_pot = jnp.zeros((cols,), jnp.float32)
    for iteration in range(ITERS):
        scores = affinity + (col_pot + log_train)[None, :]
        highest = jnp.max(scores, axis=1)
        local = highest + jnp.log(jnp.sum(jnp.exp(scores - highest[:, None]), axis=1))
        row_pot = -combine(exchange(local, "train", n_train))
        scores = affinity + (row_pot + log_gen)[:, None]
        highest = jnp.max(scores, axis=0)
        weights = jnp.exp(scores - highest[None, :])
        total = jnp.sum(weights, axis=0)
        local = highest + jnp.log(total)
        if iteration < ITERS - 1:
            col_pot = -combine(exchange(local, "gen", n_gen))
    mean = jnp.sum(weights * affinity, axis=0) / total
    small = 1 << 20
    (packed,) = call(
        pack_kernel,
        [shape(n_gen, 1, 2 * cols + LANES)],
        [local[None], mean[None], row_mass.reshape(-1, LANES)],
        limit=small,
    )
    got = lax.all_to_all(packed, "gen", 0, 0)
    col_pot, gen_mass, packed = call(
        column_kernel,
        [shape(1, cols), shape(1, LANES), shape(n_train, 1, 2 * LANES)],
        [got, col_mass[None]],
        limit=small,
    )
    got = lax.all_to_all(packed, "train", 0, 0)
    row_out, col_out, cost = call(
        outputs_kernel,
        [shape(rows // LANES, LANES), shape(1, cols), shape(1, 1)],
        [got, row_pot.reshape(-1, LANES), col_pot, gen_mass],
        limit=small,
    )
    return (row_out.reshape(rows), col_out.reshape(cols), cost.reshape(()))


def solution(mesh):
    in_specs = (P(("gen", "train"), None), P(("train", "gen"), None), P("gen"), P("train"))
    out_specs = (P("gen"), P("train"), P())

    def body(*args):
        return shards(mesh.shape["gen"], mesh.shape["train"], *args)

    return jax.shard_map(body, mesh=mesh, in_specs=in_specs, out_specs=out_specs, check_vma=False)
```

```python
import functools

import jax
import jax.numpy as jnp
from jax import lax
from jax.experimental import pallas as pl
from jax.experimental.pallas import tpu as pltpu
from jax.sharding import PartitionSpec as P

ITERS = 3


EPSILON = 0.05
LANES = 128
VMEM = pl.BlockSpec(memory_space=pltpu.VMEM)
ANY = pl.BlockSpec(memory_space=pl.ANY)


def shape(*dims):
    return jax.ShapeDtypeStruct(dims, jnp.float32)


def call(kernel, outs, ins, scratch=(), in_specs=None, out_specs=None, limit=8 << 20):
    return pl.pallas_call(
        kernel,
        out_shape=outs,
        in_specs=in_specs or [VMEM] * len(ins),
        out_specs=out_specs or [VMEM] * len(outs),
        scratch_shapes=scratch,
        compiler_params=pltpu.CompilerParams(vmem_limit_bytes=limit),
    )(*ins)


def own(shape):
    column = lax.broadcasted_iota(jnp.int32, shape, len(shape) - 1)
    share = shape[-1] // lax.axis_size("gen")
    return (column // share) % 2 == lax.axis_index("gen") % 2


def partner():
    at = lax.axis_index("train")
    return at + 1 - 2 * (at % 2)


def copies_kernel(values, mass, out, rows, row_mass, block, in_sems, sems):
    many, height, width = block.shape
    share, cols = rows.shape[0], row_mass.shape[1]
    fetches = [
        pltpu.make_async_copy(values, rows, in_sems.at[0]),
        pltpu.make_async_copy(mass, row_mass, in_sems.at[1]),
    ]
    for fetch in fetches:
        fetch.start()
    for fetch in fetches:
        fetch.wait()
    masses = jnp.concatenate([row_mass[:, at : at + width] for at in range(0, cols, width)], axis=0)
    rest = jnp.zeros((height - share - cols // width, width), jnp.float32)
    whole = jnp.concatenate([rows[...], masses, rest], axis=0)
    for k in range(many):
        block[k] = whole
    moves = [
        pltpu.make_async_copy(block, out.at[pl.ds(k * many, many)], sems.at[k]) for k in range(out.shape[0] // many)
    ]
    for move in moves:
        move.start()
    for move in moves:
        move.wait()


def affinity_kernel(scale, twice, train, train_sq, mass, out, tile_mass, log_mass):
    members, _, width = twice.shape
    share = out.shape[0] // members
    other = twice[partner(), share : share + mass.shape[1] // width, :]
    other = 0.5 * jnp.concatenate([other[k : k + 1] for k in range(other.shape[0])], axis=1)
    masses = jnp.where(own(mass.shape), mass[...], other)
    tile_mass[...] = masses
    log_mass[...] = jnp.log(masses)
    step = 8
    for start in range(0, members, step):
        part = twice[start : start + step, 0:share, :].reshape(step * share, width)
        twice_inner = lax.dot_general(
            part,
            train[...],
            (((1,), (1,)), ((), ())),
            precision=lax.Precision.HIGHEST,
            preferred_element_type=jnp.float32,
        )
        part_sq = 0.25 * jnp.sum(part * part, axis=1, keepdims=True)
        out[start * share : (start + step) * share, :] = (twice_inner - part_sq - train_sq[...]) * scale


def pack_kernel(local, mean, mass, out):
    cols = local.shape[1]
    total = jnp.sum(mass[...], axis=0, keepdims=True)
    for k in range(out.shape[0]):
        out[k, :, 0:cols] = local[...]
        out[k, :, cols : 2 * cols] = mean[...]
        out[k, :, 2 * cols :] = total


def column_kernel(got, mass, col_pot, gen_mass, out):
    count, cols = got.shape[0], mass.shape[1]
    logs = [got[k, :, 0:cols] for k in range(count)]
    highest = functools.reduce(jnp.maximum, logs)
    total = weighted = jnp.zeros_like(highest)
    sums = jnp.zeros_like(gen_mass)
    for k in range(count):
        share = jnp.exp(logs[k] - highest)
        total += share
        weighted += share * got[k, :, cols : 2 * cols]
        sums += got[k, :, 2 * cols :]
    potential = -(highest + jnp.log(total))
    col_pot[...] = potential
    gen_mass[...] = sums
    costs = mass[...] * (weighted / total)
    lanes = [slice(at, at + LANES) for at in range(0, cols, LANES)]
    cost = sum(costs[:, at] for at in lanes)
    train_mass = sum(mass[:, at] for at in lanes)
    for k in range(out.shape[0]):
        out[k, :, 0:LANES] = cost
        out[k, :, LANES : 2 * LANES] = train_mass
        out[k, :, 2 * LANES :] = potential


def outputs_kernel(got, row_pot, col_pot, gen_mass, row_out, col_out, cost_out):
    terms = [got[k, :, 0 : 2 * LANES] + got[k + 1, :, 0 : 2 * LANES] for k in range(0, got.shape[0], 2)]
    sums = functools.reduce(jnp.add, terms)
    cost = jnp.sum(sums[:, 0:LANES], axis=1, keepdims=True)
    train_total = jnp.sum(sums[:, LANES:], axis=1, keepdims=True)
    columns = jnp.where(own(col_pot.shape), col_pot[...], got[partner(), :, 2 * LANES :])
    log_train = jnp.log(train_total)
    log_gen = jnp.log(jnp.sum(gen_mass[...], axis=1, keepdims=True))
    row_out[...] = EPSILON * (row_pot[...] + (ITERS * log_train - (ITERS - 1) * log_gen))
    col_out[...] = EPSILON * (columns + ITERS * (log_gen - log_train))
    cost_out[...] = -EPSILON * cost / train_total


def exchange(values, axis, count, groups=None):
    copies = jnp.broadcast_to(values[None], (count,) + values.shape)
    return lax.all_to_all(copies, axis, 0, 0, axis_index_groups=groups)


def combine(logs):
    highest = jnp.max(logs, axis=0)
    return highest + jnp.log(jnp.sum(jnp.exp(logs - highest[None]), axis=0))


def shards(n_gen, n_train, gen_embed, train_embed, row_mass, col_mass):
    width = gen_embed.shape[1]
    rows, cols = row_mass.shape[0], col_mass.shape[0]
    both = ("gen", "train")
    groups = [
        [g * n_train + first + (g + shift) % 2 for g in range(n_gen)]
        for first in range(0, n_train, 2)
        for shift in range(2)
    ]
    small = 1 << 20
    height = gen_embed.shape[0] + 8
    many = 4
    (packed,) = call(
        copies_kernel,
        [shape(n_train, height, width)],
        [gen_embed, col_mass[None]],
        scratch=[
            pltpu.VMEM(gen_embed.shape, jnp.float32),
            pltpu.VMEM((1, cols), jnp.float32),
            pltpu.VMEM((many, height, width), jnp.float32),
            pltpu.SemaphoreType.DMA((2,)),
            pltpu.SemaphoreType.DMA((n_train // many,)),
        ],
        in_specs=[ANY, ANY],
        out_specs=[ANY],
        limit=60 << 20,
    )
    twice = 2.0 * lax.all_to_all(packed, "train", 0, 0)
    train_block = lax.all_gather(train_embed, both, axis=0, tiled=True, axis_index_groups=groups)
    train_sq = jnp.sum(train_block * train_block, axis=1)
    affinity, tile_mass, log_train = call(
        functools.partial(affinity_kernel, 1.0 / (width * EPSILON)),
        [shape(rows, cols), shape(1, cols), shape(1, cols)],
        [twice, train_block, train_sq[None], col_mass[None]],
    )
    log_train = log_train[0]

    log_gen = jnp.log(row_mass)
    col_pot = jnp.zeros((cols,), jnp.float32)
    for iteration in range(ITERS):
        scores = affinity + (col_pot + log_train)[None, :]
        highest = jnp.max(scores, axis=1)
        local = highest + jnp.log(jnp.sum(jnp.exp(scores - highest[:, None]), axis=1))
        row_pot = -combine(exchange(local, "train", n_train))
        scores = affinity + (row_pot + log_gen)[:, None]
        highest = jnp.max(scores, axis=0)
        weights = jnp.exp(scores - highest[None, :])
        total = jnp.sum(weights, axis=0)
        local = highest + jnp.log(total)
        if iteration < ITERS - 1:
            col_pot = -combine(exchange(local, both, n_gen, groups))
    mean = jnp.sum(weights * affinity, axis=0) / total
    (packed,) = call(
        pack_kernel,
        [shape(n_gen, 1, 2 * cols + LANES)],
        [local[None], mean[None], row_mass.reshape(-1, LANES)],
        limit=small,
    )
    got = lax.all_to_all(packed, both, 0, 0, axis_index_groups=groups)
    col_pot, gen_mass, packed = call(
        column_kernel,
        [shape(1, cols), shape(1, LANES), shape(n_train, 1, 2 * LANES + cols)],
        [got, tile_mass],
        limit=small,
    )
    got = lax.all_to_all(packed, "train", 0, 0)
    row_out, col_out, cost = call(
        outputs_kernel,
        [shape(rows // LANES, LANES), shape(1, cols), shape(1, 1)],
        [got, row_pot.reshape(-1, LANES), col_pot, gen_mass],
        limit=small,
    )
    return (row_out.reshape(rows), col_out.reshape(cols), cost.reshape(()))


def solution(mesh):
    in_specs = (P(("gen", "train"), None), P(("train", "gen"), None), P("gen"), P("train"))
    out_specs = (P("gen"), P("train"), P())

    def body(*args):
        return shards(mesh.shape["gen"], mesh.shape["train"], *args)

    return jax.shard_map(body, mesh=mesh, in_specs=in_specs, out_specs=out_specs, check_vma=False)
```

```python
import functools

import jax
import jax.numpy as jnp
from jax import lax
from jax.experimental import pallas as pl
from jax.experimental.pallas import tpu as pltpu
from jax.sharding import PartitionSpec as P

ITERS = 3


EPSILON = 0.05
LANES = 128
VMEM = pl.BlockSpec(memory_space=pltpu.VMEM)
ANY = pl.BlockSpec(memory_space=pl.ANY)


def shape(*dims):
    return jax.ShapeDtypeStruct(dims, jnp.float32)


def call(kernel, outs, ins, scratch=(), in_specs=None, out_specs=None, limit=8 << 20):
    return pl.pallas_call(
        kernel,
        out_shape=outs,
        in_specs=in_specs or [VMEM] * len(ins),
        out_specs=out_specs or [VMEM] * len(outs),
        scratch_shapes=scratch,
        compiler_params=pltpu.CompilerParams(vmem_limit_bytes=limit),
    )(*ins)


def own(shape):
    column = lax.broadcasted_iota(jnp.int32, shape, len(shape) - 1)
    share = shape[-1] // lax.axis_size("gen")
    return (column // share) % 2 == lax.axis_index("gen") % 2


def partner():
    at = lax.axis_index("train")
    return at + 1 - 2 * (at % 2)


def copies_kernel(values, mass, out, rows, row_mass, block, in_sems, sems):
    many, height, width = block.shape
    share, cols = rows.shape[0], row_mass.shape[1]
    fetches = [
        pltpu.make_async_copy(values, rows, in_sems.at[0]),
        pltpu.make_async_copy(mass, row_mass, in_sems.at[1]),
    ]
    for fetch in fetches:
        fetch.start()
    for fetch in fetches:
        fetch.wait()
    masses = jnp.concatenate([row_mass[:, at : at + width] for at in range(0, cols, width)], axis=0)
    rest = jnp.zeros((height - share - cols // width, width), jnp.float32)
    whole = jnp.concatenate([rows[...], masses, rest], axis=0)
    for k in range(many):
        block[k] = whole
    moves = [
        pltpu.make_async_copy(block, out.at[pl.ds(k * many, many)], sems.at[k]) for k in range(out.shape[0] // many)
    ]
    for move in moves:
        move.start()
    for move in moves:
        move.wait()


def halves(values):
    high = values.astype(jnp.bfloat16)
    return high, (values - high.astype(jnp.float32)).astype(jnp.bfloat16)


def affinity_kernel(scale, twice, train, train_sq, mass, out, tile_mass, log_mass):
    members, _, width = twice.shape
    share = out.shape[0] // members
    other = twice[partner(), share : share + mass.shape[1] // width, :]
    other = 0.5 * jnp.concatenate([other[k : k + 1] for k in range(other.shape[0])], axis=1)
    masses = jnp.where(own(mass.shape), mass[...], other)
    tile_mass[...] = masses
    log_mass[...] = jnp.log(masses)
    columns = halves(train[...])
    step = 8
    for start in range(0, members, step):
        part = twice[start : start + step, 0:share, :].reshape(step * share, width)
        rows = halves(part)
        twice_inner = sum(
            lax.dot_general(left, right, (((1,), (1,)), ((), ())), preferred_element_type=jnp.float32)
            for left in reversed(rows)
            for right in reversed(columns)
        )
        part_sq = 0.25 * jnp.sum(part * part, axis=1, keepdims=True)
        out[start * share : (start + step) * share, :] = (twice_inner - part_sq - train_sq[...]) * scale


def pack_kernel(local, mean, mass, out):
    cols = local.shape[1]
    total = jnp.sum(mass[...], axis=0, keepdims=True)
    for k in range(out.shape[0]):
        out[k, :, 0:cols] = local[...]
        out[k, :, cols : 2 * cols] = mean[...]
        out[k, :, 2 * cols :] = total


def column_kernel(got, mass, col_pot, gen_mass, out):
    count, cols = got.shape[0], mass.shape[1]
    logs = [got[k, :, 0:cols] for k in range(count)]
    highest = functools.reduce(jnp.maximum, logs)
    total = weighted = jnp.zeros_like(highest)
    sums = jnp.zeros_like(gen_mass)
    for k in range(count):
        share = jnp.exp(logs[k] - highest)
        total += share
        weighted += share * got[k, :, cols : 2 * cols]
        sums += got[k, :, 2 * cols :]
    potential = -(highest + jnp.log(total))
    col_pot[...] = potential
    gen_mass[...] = sums
    costs = mass[...] * (weighted / total)
    lanes = [slice(at, at + LANES) for at in range(0, cols, LANES)]
    cost = sum(costs[:, at] for at in lanes)
    train_mass = sum(mass[:, at] for at in lanes)
    for k in range(out.shape[0]):
        out[k, :, 0:LANES] = cost
        out[k, :, LANES : 2 * LANES] = train_mass
        out[k, :, 2 * LANES :] = potential


def outputs_kernel(got, row_pot, col_pot, gen_mass, row_out, col_out, cost_out):
    terms = [got[k, :, 0 : 2 * LANES] + got[k + 1, :, 0 : 2 * LANES] for k in range(0, got.shape[0], 2)]
    sums = functools.reduce(jnp.add, terms)
    cost = jnp.sum(sums[:, 0:LANES], axis=1, keepdims=True)
    train_total = jnp.sum(sums[:, LANES:], axis=1, keepdims=True)
    columns = jnp.where(own(col_pot.shape), col_pot[...], got[partner(), :, 2 * LANES :])
    log_train = jnp.log(train_total)
    log_gen = jnp.log(jnp.sum(gen_mass[...], axis=1, keepdims=True))
    row_out[...] = EPSILON * (row_pot[...] + (ITERS * log_train - (ITERS - 1) * log_gen))
    col_out[...] = EPSILON * (columns + ITERS * (log_gen - log_train))
    cost_out[...] = -EPSILON * cost / train_total


def exchange(values, axis, count, groups=None):
    copies = jnp.broadcast_to(values[None], (count,) + values.shape)
    return lax.all_to_all(copies, axis, 0, 0, axis_index_groups=groups)


def combine(logs):
    highest = jnp.max(logs, axis=0)
    return highest + jnp.log(jnp.sum(jnp.exp(logs - highest[None]), axis=0))


def shards(n_gen, n_train, gen_embed, train_embed, row_mass, col_mass):
    width = gen_embed.shape[1]
    rows, cols = row_mass.shape[0], col_mass.shape[0]
    both = ("gen", "train")
    groups = [
        [g * n_train + first + (g + shift) % 2 for g in range(n_gen)]
        for first in range(0, n_train, 2)
        for shift in range(2)
    ]
    small = 1 << 20
    height = gen_embed.shape[0] + 8
    many = 4
    (packed,) = call(
        copies_kernel,
        [shape(n_train, height, width)],
        [gen_embed, col_mass[None]],
        scratch=[
            pltpu.VMEM(gen_embed.shape, jnp.float32),
            pltpu.VMEM((1, cols), jnp.float32),
            pltpu.VMEM((many, height, width), jnp.float32),
            pltpu.SemaphoreType.DMA((2,)),
            pltpu.SemaphoreType.DMA((n_train // many,)),
        ],
        in_specs=[ANY, ANY],
        out_specs=[ANY],
        limit=60 << 20,
    )
    twice = 2.0 * lax.all_to_all(packed, "train", 0, 0)
    train_block = lax.all_gather(train_embed, both, axis=0, tiled=True, axis_index_groups=groups)
    train_sq = jnp.sum(train_block * train_block, axis=1)
    affinity, tile_mass, log_train = call(
        functools.partial(affinity_kernel, 1.0 / (width * EPSILON)),
        [shape(rows, cols), shape(1, cols), shape(1, cols)],
        [twice, train_block, train_sq[None], col_mass[None]],
    )
    log_train = log_train[0]

    log_gen = jnp.log(row_mass)
    col_pot = jnp.zeros((cols,), jnp.float32)
    for iteration in range(ITERS):
        scores = affinity + (col_pot + log_train)[None, :]
        highest = jnp.max(scores, axis=1)
        local = highest + jnp.log(jnp.sum(jnp.exp(scores - highest[:, None]), axis=1))
        row_pot = -combine(exchange(local, "train", n_train))
        scores = affinity + (row_pot + log_gen)[:, None]
        highest = jnp.max(scores, axis=0)
        weights = jnp.exp(scores - highest[None, :])
        total = jnp.sum(weights, axis=0)
        local = highest + jnp.log(total)
        if iteration < ITERS - 1:
            col_pot = -combine(exchange(local, both, n_gen, groups))
    mean = jnp.sum(weights * affinity, axis=0) / total
    (packed,) = call(
        pack_kernel,
        [shape(n_gen, 1, 2 * cols + LANES)],
        [local[None], mean[None], row_mass.reshape(-1, LANES)],
        limit=small,
    )
    got = lax.all_to_all(packed, both, 0, 0, axis_index_groups=groups)
    col_pot, gen_mass, packed = call(
        column_kernel,
        [shape(1, cols), shape(1, LANES), shape(n_train, 1, 2 * LANES + cols)],
        [got, tile_mass],
        limit=small,
    )
    got = lax.all_to_all(packed, "train", 0, 0)
    row_out, col_out, cost = call(
        outputs_kernel,
        [shape(rows // LANES, LANES), shape(1, cols), shape(1, 1)],
        [got, row_pot.reshape(-1, LANES), col_pot, gen_mass],
        limit=small,
    )
    return (row_out.reshape(rows), col_out.reshape(cols), cost.reshape(()))


def solution(mesh):
    in_specs = (P(("gen", "train"), None), P(("train", "gen"), None), P("gen"), P("train"))
    out_specs = (P("gen"), P("train"), P())

    def body(*args):
        return shards(mesh.shape["gen"], mesh.shape["train"], *args)

    return jax.shard_map(body, mesh=mesh, in_specs=in_specs, out_specs=out_specs, check_vma=False)
```

```python
import functools

import jax
import jax.numpy as jnp
from jax import lax
from jax.experimental import pallas as pl
from jax.experimental.pallas import tpu as pltpu
from jax.sharding import PartitionSpec as P

ITERS = 3


EPSILON = 0.05
LANES = 128
VMEM = pl.BlockSpec(memory_space=pltpu.VMEM)
ANY = pl.BlockSpec(memory_space=pl.ANY)


def shape(*dims):
    return jax.ShapeDtypeStruct(dims, jnp.float32)


def call(kernel, outs, ins, scratch=(), in_specs=None, out_specs=None, limit=8 << 20):
    return pl.pallas_call(
        kernel,
        out_shape=outs,
        in_specs=in_specs or [VMEM] * len(ins),
        out_specs=out_specs or [VMEM] * len(outs),
        scratch_shapes=scratch,
        compiler_params=pltpu.CompilerParams(vmem_limit_bytes=limit),
    )(*ins)


def own(shape):
    column = lax.broadcasted_iota(jnp.int32, shape, len(shape) - 1)
    share = shape[-1] // lax.axis_size("gen")
    return (column // share) % 2 == lax.axis_index("gen") % 2


def partner():
    at = lax.axis_index("train")
    return at + 1 - 2 * (at % 2)


def copies_kernel(values, mass, out, rows, row_mass, block, in_sems, sems):
    many, height, width = block.shape
    share, cols = rows.shape[0], row_mass.shape[1]
    fetches = [
        pltpu.make_async_copy(values, rows, in_sems.at[0]),
        pltpu.make_async_copy(mass, row_mass, in_sems.at[1]),
    ]
    for fetch in fetches:
        fetch.start()
    for fetch in fetches:
        fetch.wait()
    masses = jnp.concatenate([row_mass[:, at : at + width] for at in range(0, cols, width)], axis=0)
    rest = jnp.zeros((height - share - cols // width, width), jnp.float32)
    whole = jnp.concatenate([rows[...], masses, rest], axis=0)
    for k in range(many):
        block[k] = whole
    moves = [
        pltpu.make_async_copy(block, out.at[pl.ds(k * many, many)], sems.at[k]) for k in range(out.shape[0] // many)
    ]
    for move in moves:
        move.start()
    for move in moves:
        move.wait()


def halves(values):
    high = values.astype(jnp.bfloat16)
    return high, (values - high.astype(jnp.float32)).astype(jnp.bfloat16)


def combined(got, cols):
    logs = [got[k, :, 0:cols] for k in range(got.shape[0])]
    highest = functools.reduce(jnp.maximum, logs)
    return highest + jnp.log(sum(jnp.exp(log - highest) for log in logs))


def row_logs(block, weights):
    pieces = []
    for at in range(0, block.shape[0], LANES):
        scores = block[at : at + LANES, :] + weights
        highest = jnp.max(scores, axis=1, keepdims=True)
        total = jnp.sum(jnp.exp(scores - highest), axis=1, keepdims=True)
        pieces.append(jnp.broadcast_to(highest + jnp.log(total), (LANES, LANES)).T[0:1, :])
    return pieces


def send(pieces, out):
    whole = jnp.concatenate(pieces, axis=1)
    for k in range(out.shape[0]):
        out[k] = whole


def train_kernel(got, log_train, affinity, out):
    send(row_logs(affinity, log_train[...] - combined(got, log_train.shape[1])), out)


def gen_kernel(last, got, mass, affinity, *outs):
    rows, cols = affinity.shape
    out, offsets = outs[-2:]
    potential = -combined(got, rows)
    if last:
        outs[0][...] = potential
    weights = potential + jnp.log(mass[...])
    lanes = cols // LANES
    sub = 8

    def fold(reduce, block):
        return reduce(block.reshape(LANES // sub, sub, cols), axis=0)

    def scores(at):
        return affinity[at : at + LANES, :] + jnp.concatenate([offsets[at : at + LANES, :]] * lanes, axis=1)

    highest = None
    for at in range(0, rows, LANES):
        offsets[at : at + LANES, :] = jnp.broadcast_to(weights[:, at : at + LANES], (LANES, LANES)).T
        part = fold(jnp.max, scores(at))
        highest = part if highest is None else jnp.maximum(highest, part)
    highest = jnp.max(highest, axis=0, keepdims=True)
    total = mean = jnp.zeros((sub, cols), jnp.float32)
    for at in range(0, rows, LANES):
        share = jnp.exp(scores(at) - highest)
        total += fold(jnp.sum, share)
        if last:
            mean += fold(jnp.sum, share * affinity[at : at + LANES, :])
    total = jnp.sum(total, axis=0, keepdims=True)
    logs = highest + jnp.log(total)
    if last:
        mean = jnp.sum(mean, axis=0, keepdims=True) / total
        masses = sum(mass[:, at : at + LANES] for at in range(0, rows, LANES))
        send([logs, mean, masses], out)
    else:
        send([logs], out)


def affinity_kernel(scale, twice, train, train_sq, out, tile_mass, log_mass, logs):
    members, _, width = twice.shape
    share = out.shape[0] // members
    cols = out.shape[1]

    def mass_of(member):
        held = twice[member, share : share + cols // width, :]
        return 0.5 * jnp.concatenate([held[k : k + 1] for k in range(cols // width)], axis=1)

    masses = jnp.where(own((1, cols)), mass_of(lax.axis_index("train")), mass_of(partner()))
    tile_mass[...] = masses
    weights = jnp.log(masses)
    log_mass[...] = weights
    columns = halves(train[...])
    pieces = []
    step = 8
    for start in range(0, members, step):
        part = twice[start : start + step, 0:share, :].reshape(step * share, width)
        rows = halves(part)
        twice_inner = sum(
            lax.dot_general(left, right, (((1,), (1,)), ((), ())), preferred_element_type=jnp.float32)
            for left in reversed(rows)
            for right in reversed(columns)
        )
        part_sq = 0.25 * jnp.sum(part * part, axis=1, keepdims=True)
        block = (twice_inner - part_sq - train_sq[...]) * scale
        out[start * share : (start + step) * share, :] = block
        pieces += row_logs(block, weights)
    send(pieces, logs)


def column_kernel(got, mass, col_pot, gen_mass, out):
    count, cols = got.shape[0], mass.shape[1]
    logs = [got[k, :, 0:cols] for k in range(count)]
    highest = functools.reduce(jnp.maximum, logs)
    total = weighted = jnp.zeros_like(highest)
    sums = jnp.zeros_like(gen_mass)
    for k in range(count):
        share = jnp.exp(logs[k] - highest)
        total += share
        weighted += share * got[k, :, cols : 2 * cols]
        sums += got[k, :, 2 * cols :]
    potential = -(highest + jnp.log(total))
    col_pot[...] = potential
    gen_mass[...] = sums
    costs = mass[...] * (weighted / total)
    lanes = [slice(at, at + LANES) for at in range(0, cols, LANES)]
    cost = sum(costs[:, at] for at in lanes)
    train_mass = sum(mass[:, at] for at in lanes)
    for k in range(out.shape[0]):
        out[k, :, 0:LANES] = cost
        out[k, :, LANES : 2 * LANES] = train_mass
        out[k, :, 2 * LANES :] = potential


def outputs_kernel(got, row_pot, col_pot, gen_mass, row_out, col_out, cost_out):
    terms = [got[k, :, 0 : 2 * LANES] + got[k + 1, :, 0 : 2 * LANES] for k in range(0, got.shape[0], 2)]
    sums = functools.reduce(jnp.add, terms)
    cost = jnp.sum(sums[:, 0:LANES], axis=1, keepdims=True)
    train_total = jnp.sum(sums[:, LANES:], axis=1, keepdims=True)
    columns = jnp.where(own(col_pot.shape), col_pot[...], got[partner(), :, 2 * LANES :])
    log_train = jnp.log(train_total)
    log_gen = jnp.log(jnp.sum(gen_mass[...], axis=1, keepdims=True))
    row_out[...] = EPSILON * (row_pot[...] + (ITERS * log_train - (ITERS - 1) * log_gen))
    col_out[...] = EPSILON * (columns + ITERS * (log_gen - log_train))
    cost_out[...] = -EPSILON * cost / train_total


def shards(n_gen, n_train, gen_embed, train_embed, row_mass, col_mass):
    width = gen_embed.shape[1]
    rows, cols = row_mass.shape[0], col_mass.shape[0]
    both = ("gen", "train")
    groups = [
        [g * n_train + first + (g + shift) % 2 for g in range(n_gen)]
        for first in range(0, n_train, 2)
        for shift in range(2)
    ]
    small = 1 << 20
    height = gen_embed.shape[0] + 8
    many = 4
    (packed,) = call(
        copies_kernel,
        [shape(n_train, height, width)],
        [gen_embed, col_mass[None]],
        scratch=[
            pltpu.VMEM(gen_embed.shape, jnp.float32),
            pltpu.VMEM((1, cols), jnp.float32),
            pltpu.VMEM((many, height, width), jnp.float32),
            pltpu.SemaphoreType.DMA((2,)),
            pltpu.SemaphoreType.DMA((n_train // many,)),
        ],
        in_specs=[ANY, ANY],
        out_specs=[ANY],
        limit=60 << 20,
    )
    twice = 2.0 * lax.all_to_all(packed, "train", 0, 0)
    train_block = lax.all_gather(train_embed, both, axis=0, tiled=True, axis_index_groups=groups)
    train_sq = jnp.sum(train_block * train_block, axis=1)
    affinity, tile_mass, log_train, packed = call(
        functools.partial(affinity_kernel, 1.0 / (width * EPSILON)),
        [shape(rows, cols), shape(1, cols), shape(1, cols), shape(n_train, 1, rows)],
        [twice, train_block, train_sq[None]],
    )

    for iteration in range(ITERS):
        last = iteration == ITERS - 1
        got = lax.all_to_all(packed, "train", 0, 0)
        *row_pot, packed = call(
            functools.partial(gen_kernel, last),
            [shape(1, rows), shape(n_gen, 1, 2 * cols + LANES)] if last else [shape(n_gen, 1, cols)],
            [got, row_mass[None], affinity],
            scratch=[pltpu.VMEM((rows, LANES), jnp.float32)],
        )
        got = lax.all_to_all(packed, both, 0, 0, axis_index_groups=groups)
        if not last:
            (packed,) = call(train_kernel, [shape(n_train, 1, rows)], [got, log_train, affinity])
    col_pot, gen_mass, packed = call(
        column_kernel,
        [shape(1, cols), shape(1, LANES), shape(n_train, 1, 2 * LANES + cols)],
        [got, tile_mass],
        limit=small,
    )
    got = lax.all_to_all(packed, "train", 0, 0)
    row_out, col_out, cost = call(
        outputs_kernel,
        [shape(1, rows), shape(1, cols), shape(1, 1)],
        [got, *row_pot, col_pot, gen_mass],
        limit=small,
    )
    return (row_out.reshape(rows), col_out.reshape(cols), cost.reshape(()))


def solution(mesh):
    in_specs = (P(("gen", "train"), None), P(("train", "gen"), None), P("gen"), P("train"))
    out_specs = (P("gen"), P("train"), P())

    def body(*args):
        return shards(mesh.shape["gen"], mesh.shape["train"], *args)

    return jax.shard_map(body, mesh=mesh, in_specs=in_specs, out_specs=out_specs, check_vma=False)
```

```python
import functools

import jax
import jax.numpy as jnp
from jax import lax
from jax.experimental import pallas as pl
from jax.experimental.pallas import tpu as pltpu
from jax.sharding import PartitionSpec as P

ITERS = 3


EPSILON = 0.05
LANES = 128
VMEM = pl.BlockSpec(memory_space=pltpu.VMEM)
ANY = pl.BlockSpec(memory_space=pl.ANY)


def shape(*dims):
    return jax.ShapeDtypeStruct(dims, jnp.float32)


def call(kernel, outs, ins, scratch=(), in_specs=None, out_specs=None, limit=8 << 20):
    return pl.pallas_call(
        kernel,
        out_shape=outs,
        in_specs=in_specs or [VMEM] * len(ins),
        out_specs=out_specs or [VMEM] * len(outs),
        scratch_shapes=scratch,
        compiler_params=pltpu.CompilerParams(vmem_limit_bytes=limit),
    )(*ins)


def own(shape):
    column = lax.broadcasted_iota(jnp.int32, shape, len(shape) - 1)
    share = shape[-1] // lax.axis_size("gen")
    return (column // share) % 2 == lax.axis_index("gen") % 2


def partner():
    at = lax.axis_index("train")
    return at + 1 - 2 * (at % 2)


def copies_kernel(values, mass, out, rows, row_mass, block, in_sems, sems):
    many, height, width = block.shape
    share, cols = rows.shape[0], row_mass.shape[1]
    fetches = [
        pltpu.make_async_copy(values, rows, in_sems.at[0]),
        pltpu.make_async_copy(mass, row_mass, in_sems.at[1]),
    ]
    for fetch in fetches:
        fetch.start()
    for fetch in fetches:
        fetch.wait()
    masses = jnp.concatenate([row_mass[:, at : at + width] for at in range(0, cols, width)], axis=0)
    rest = jnp.zeros((height - share - cols // width, width), jnp.float32)
    whole = jnp.concatenate([rows[...], masses, rest], axis=0)
    for k in range(many):
        block[k] = whole
    moves = [
        pltpu.make_async_copy(block, out.at[pl.ds(k * many, many)], sems.at[k]) for k in range(out.shape[0] // many)
    ]
    for move in moves:
        move.start()
    for move in moves:
        move.wait()


def halves(values):
    high = values.astype(jnp.bfloat16)
    return high, (values - high.astype(jnp.float32)).astype(jnp.bfloat16)


def combined(got, cols):
    logs = [got[k, :, 0:cols] for k in range(got.shape[0])]
    highest = functools.reduce(jnp.maximum, logs)
    return highest + jnp.log(sum(jnp.exp(log - highest) for log in logs))


def row_logs(block, weights):
    starts = range(0, block.shape[0], LANES)

    def scores(at):
        return block[at : at + LANES, :] + weights

    highest = [jnp.max(scores(at), axis=1, keepdims=True) for at in starts]
    totals = [jnp.sum(jnp.exp(scores(at) - high), axis=1, keepdims=True) for at, high in zip(starts, highest)]
    logs = [high + jnp.log(total) for high, total in zip(highest, totals)]
    return [jnp.broadcast_to(log, (LANES, LANES)).T[0:1, :] for log in logs]


def send(pieces, out):
    whole = jnp.concatenate(pieces, axis=1)
    for k in range(out.shape[0]):
        out[k] = whole


def train_kernel(got, log_train, affinity, out):
    send(row_logs(affinity, log_train[...] - combined(got, log_train.shape[1])), out)


def gen_kernel(last, got, mass, affinity, *outs):
    rows, cols = affinity.shape
    out, offsets = outs[-2:]
    potential = -combined(got, rows)
    if last:
        outs[0][...] = potential
    weights = potential + jnp.log(mass[...])
    lanes = cols // LANES
    sub = 8

    def fold(reduce, block):
        return reduce(block.reshape(LANES // sub, sub, cols), axis=0)

    def scores(at):
        return affinity[at : at + LANES, :] + jnp.concatenate([offsets[at : at + LANES, :]] * lanes, axis=1)

    highest = None
    for at in range(0, rows, LANES):
        offsets[at : at + LANES, :] = jnp.broadcast_to(weights[:, at : at + LANES], (LANES, LANES)).T
        part = fold(jnp.max, scores(at))
        highest = part if highest is None else jnp.maximum(highest, part)
    highest = jnp.max(highest, axis=0, keepdims=True)
    total = mean = jnp.zeros((sub, cols), jnp.float32)
    for at in range(0, rows, LANES):
        share = jnp.exp(scores(at) - highest)
        total += fold(jnp.sum, share)
        if last:
            mean += fold(jnp.sum, share * affinity[at : at + LANES, :])
    total = jnp.sum(total, axis=0, keepdims=True)
    logs = highest + jnp.log(total)
    if last:
        mean = jnp.sum(mean, axis=0, keepdims=True) / total
        masses = sum(mass[:, at : at + LANES] for at in range(0, rows, LANES))
        send([logs, mean, masses], out)
    else:
        send([logs], out)


def affinity_kernel(scale, twice, train, train_sq, out, tile_mass, log_mass, logs):
    members, _, width = twice.shape
    share = out.shape[0] // members
    cols = out.shape[1]

    def mass_of(member):
        held = twice[member, share : share + cols // width, :]
        return 0.5 * jnp.concatenate([held[k : k + 1] for k in range(cols // width)], axis=1)

    masses = jnp.where(own((1, cols)), mass_of(lax.axis_index("train")), mass_of(partner()))
    tile_mass[...] = masses
    weights = jnp.log(masses)
    log_mass[...] = weights
    columns = halves(train[...])
    pieces = []
    step = 8
    for start in range(0, members, step):
        part = twice[start : start + step, 0:share, :].reshape(step * share, width)
        rows = halves(part)
        twice_inner = sum(
            lax.dot_general(left, right, (((1,), (1,)), ((), ())), preferred_element_type=jnp.float32)
            for left in reversed(rows)
            for right in reversed(columns)
        )
        part_sq = 0.25 * jnp.sum(part * part, axis=1, keepdims=True)
        block = (twice_inner - part_sq - train_sq[...]) * scale
        out[start * share : (start + step) * share, :] = block
        pieces += row_logs(block, weights)
    send(pieces, logs)


def column_kernel(got, mass, col_pot, gen_mass, out):
    count, cols = got.shape[0], mass.shape[1]
    logs = [got[k, :, 0:cols] for k in range(count)]
    highest = functools.reduce(jnp.maximum, logs)
    total = weighted = jnp.zeros_like(highest)
    sums = jnp.zeros_like(gen_mass)
    for k in range(count):
        share = jnp.exp(logs[k] - highest)
        total += share
        weighted += share * got[k, :, cols : 2 * cols]
        sums += got[k, :, 2 * cols :]
    potential = -(highest + jnp.log(total))
    col_pot[...] = potential
    gen_mass[...] = sums
    costs = mass[...] * (weighted / total)
    lanes = [slice(at, at + LANES) for at in range(0, cols, LANES)]
    cost = sum(costs[:, at] for at in lanes)
    train_mass = sum(mass[:, at] for at in lanes)
    for k in range(out.shape[0]):
        out[k, :, 0:LANES] = cost
        out[k, :, LANES : 2 * LANES] = train_mass
        out[k, :, 2 * LANES :] = potential


def outputs_kernel(got, row_pot, col_pot, gen_mass, row_out, col_out, cost_out):
    terms = [got[k, :, 0 : 2 * LANES] + got[k + 1, :, 0 : 2 * LANES] for k in range(0, got.shape[0], 2)]
    sums = functools.reduce(jnp.add, terms)
    cost = jnp.sum(sums[:, 0:LANES], axis=1, keepdims=True)
    train_total = jnp.sum(sums[:, LANES:], axis=1, keepdims=True)
    columns = jnp.where(own(col_pot.shape), col_pot[...], got[partner(), :, 2 * LANES :])
    log_train = jnp.log(train_total)
    log_gen = jnp.log(jnp.sum(gen_mass[...], axis=1, keepdims=True))
    row_out[...] = EPSILON * (row_pot[...] + (ITERS * log_train - (ITERS - 1) * log_gen))
    col_out[...] = EPSILON * (columns + ITERS * (log_gen - log_train))
    cost_out[...] = -EPSILON * cost / train_total


def shards(n_gen, n_train, gen_embed, train_embed, row_mass, col_mass):
    width = gen_embed.shape[1]
    rows, cols = row_mass.shape[0], col_mass.shape[0]
    both = ("gen", "train")
    groups = [
        [g * n_train + first + (g + shift) % 2 for g in range(n_gen)]
        for first in range(0, n_train, 2)
        for shift in range(2)
    ]
    small = 1 << 20
    height = gen_embed.shape[0] + 8
    many = 4
    (packed,) = call(
        copies_kernel,
        [shape(n_train, height, width)],
        [gen_embed, col_mass[None]],
        scratch=[
            pltpu.VMEM(gen_embed.shape, jnp.float32),
            pltpu.VMEM((1, cols), jnp.float32),
            pltpu.VMEM((many, height, width), jnp.float32),
            pltpu.SemaphoreType.DMA((2,)),
            pltpu.SemaphoreType.DMA((n_train // many,)),
        ],
        in_specs=[ANY, ANY],
        out_specs=[ANY],
        limit=60 << 20,
    )
    twice = 2.0 * lax.all_to_all(packed, "train", 0, 0)
    train_block = lax.all_gather(train_embed, both, axis=0, tiled=True, axis_index_groups=groups)
    train_sq = jnp.sum(train_block * train_block, axis=1)
    affinity, tile_mass, log_train, packed = call(
        functools.partial(affinity_kernel, 1.0 / (width * EPSILON)),
        [shape(rows, cols), shape(1, cols), shape(1, cols), shape(n_train, 1, rows)],
        [twice, train_block, train_sq[None]],
    )

    for iteration in range(ITERS):
        last = iteration == ITERS - 1
        got = lax.all_to_all(packed, "train", 0, 0)
        *row_pot, packed = call(
            functools.partial(gen_kernel, last),
            [shape(1, rows), shape(n_gen, 1, 2 * cols + LANES)] if last else [shape(n_gen, 1, cols)],
            [got, row_mass[None], affinity],
            scratch=[pltpu.VMEM((rows, LANES), jnp.float32)],
        )
        got = lax.all_to_all(packed, both, 0, 0, axis_index_groups=groups)
        if not last:
            (packed,) = call(train_kernel, [shape(n_train, 1, rows)], [got, log_train, affinity])
    col_pot, gen_mass, packed = call(
        column_kernel,
        [shape(1, cols), shape(1, LANES), shape(n_train, 1, 2 * LANES + cols)],
        [got, tile_mass],
        limit=small,
    )
    got = lax.all_to_all(packed, "train", 0, 0)
    row_out, col_out, cost = call(
        outputs_kernel,
        [shape(1, rows), shape(1, cols), shape(1, 1)],
        [got, *row_pot, col_pot, gen_mass],
        limit=small,
    )
    return (row_out.reshape(rows), col_out.reshape(cols), cost.reshape(()))


def solution(mesh):
    in_specs = (P(("gen", "train"), None), P(("train", "gen"), None), P("gen"), P("train"))
    out_specs = (P("gen"), P("train"), P())

    def body(*args):
        return shards(mesh.shape["gen"], mesh.shape["train"], *args)

    return jax.shard_map(body, mesh=mesh, in_specs=in_specs, out_specs=out_specs, check_vma=False)
```

```python
import functools

import jax
import jax.numpy as jnp
from jax import lax
from jax.experimental import pallas as pl
from jax.experimental.pallas import tpu as pltpu
from jax.sharding import PartitionSpec as P

ITERS = 3


EPSILON = 0.05
LANES = 128
VMEM = pl.BlockSpec(memory_space=pltpu.VMEM)
ANY = pl.BlockSpec(memory_space=pl.ANY)


def shape(*dims):
    return jax.ShapeDtypeStruct(dims, jnp.float32)


def call(kernel, outs, ins, scratch=(), in_specs=None, out_specs=None, limit=8 << 20):
    return pl.pallas_call(
        kernel,
        out_shape=outs,
        in_specs=in_specs or [VMEM] * len(ins),
        out_specs=out_specs or [VMEM] * len(outs),
        scratch_shapes=scratch,
        compiler_params=pltpu.CompilerParams(vmem_limit_bytes=limit),
    )(*ins)


def own(shape):
    column = lax.broadcasted_iota(jnp.int32, shape, len(shape) - 1)
    share = shape[-1] // lax.axis_size("gen")
    return (column // share) % 2 == lax.axis_index("gen") % 2


def partner():
    at = lax.axis_index("train")
    return at + 1 - 2 * (at % 2)


def copies_kernel(values, mass, out, rows, row_mass, block, in_sems, sems):
    many, height, width = block.shape
    share, cols = rows.shape[0], row_mass.shape[1]
    fetches = [
        pltpu.make_async_copy(values, rows, in_sems.at[0]),
        pltpu.make_async_copy(mass, row_mass, in_sems.at[1]),
    ]
    for fetch in fetches:
        fetch.start()
    for fetch in fetches:
        fetch.wait()
    masses = jnp.concatenate([row_mass[:, at : at + width] for at in range(0, cols, width)], axis=0)
    rest = jnp.zeros((height - share - cols // width, width), jnp.float32)
    whole = jnp.concatenate([rows[...], masses, rest], axis=0)
    for k in range(many):
        block[k] = whole
    moves = [
        pltpu.make_async_copy(block, out.at[pl.ds(k * many, many)], sems.at[k]) for k in range(out.shape[0] // many)
    ]
    for move in moves:
        move.start()
    for move in moves:
        move.wait()


def halves(values):
    high = values.astype(jnp.bfloat16)
    return high, (values - high.astype(jnp.float32)).astype(jnp.bfloat16)


def combined(got, cols):
    logs = [got[k, :, 0:cols] for k in range(got.shape[0])]
    highest = functools.reduce(jnp.maximum, logs)
    return highest + jnp.log(sum(jnp.exp(log - highest) for log in logs))


def row_logs(block, weights):
    starts = range(0, block.shape[0], LANES)

    def scores(at):
        return block[at : at + LANES, :] + weights

    highest = [jnp.max(scores(at), axis=1, keepdims=True) for at in starts]
    totals = [jnp.sum(jnp.exp(scores(at) - high), axis=1, keepdims=True) for at, high in zip(starts, highest)]
    logs = [high + jnp.log(total) for high, total in zip(highest, totals)]
    return [jnp.broadcast_to(log, (LANES, LANES)).T[0:1, :] for log in logs]


def send(pieces, out):
    whole = jnp.concatenate(pieces, axis=1)
    for k in range(out.shape[0]):
        out[k] = whole


def train_kernel(got, log_train, affinity, out):
    send(row_logs(affinity, log_train[...] - combined(got, log_train.shape[1])), out)


def gen_kernel(last, got, mass, affinity, *outs):
    rows, cols = affinity.shape
    out, offsets = outs[-2:]
    potential = -combined(got, rows)
    if last:
        outs[0][...] = potential
    weights = potential + jnp.log(mass[...])
    lanes = cols // LANES
    sub = 8

    def fold(reduce, block):
        return reduce(block.reshape(LANES // sub, sub, cols), axis=0)

    def scores(at):
        return affinity[at : at + LANES, :] + jnp.concatenate([offsets[at : at + LANES, :]] * lanes, axis=1)

    highest = None
    for at in range(0, rows, LANES):
        offsets[at : at + LANES, :] = jnp.broadcast_to(weights[:, at : at + LANES], (LANES, LANES)).T
        part = fold(jnp.max, scores(at))
        highest = part if highest is None else jnp.maximum(highest, part)
    highest = jnp.max(highest, axis=0, keepdims=True)
    total = mean = jnp.zeros((sub, cols), jnp.float32)
    for at in range(0, rows, LANES):
        share = jnp.exp(scores(at) - highest)
        total += fold(jnp.sum, share)
        if last:
            mean += fold(jnp.sum, share * affinity[at : at + LANES, :])
    total = jnp.sum(total, axis=0, keepdims=True)
    logs = highest + jnp.log(total)
    if last:
        mean = jnp.sum(mean, axis=0, keepdims=True) / total
        masses = sum(mass[:, at : at + LANES] for at in range(0, rows, LANES))
        send([logs, mean, masses], out)
    else:
        send([logs], out)


def affinity_kernel(scale, twice, train, out, tile_mass, log_mass, logs):
    members, _, width = twice.shape
    share = out.shape[0] // members
    cols = out.shape[1]

    def mass_of(member):
        held = twice[member, share : share + cols // width, :]
        return 0.5 * jnp.concatenate([held[k : k + 1] for k in range(cols // width)], axis=1)

    masses = jnp.where(own((1, cols)), mass_of(lax.axis_index("train")), mass_of(partner()))
    tile_mass[...] = masses
    weights = jnp.log(masses)
    log_mass[...] = weights
    columns = halves(train[...])
    squares = [train[at : at + LANES, :] * train[at : at + LANES, :] for at in range(0, cols, LANES)]
    squares = [jnp.sum(part, axis=1, keepdims=True) for part in squares]
    train_sq = jnp.concatenate([jnp.broadcast_to(part, (LANES, LANES)).T[0:1, :] for part in squares], axis=1)
    pieces = []
    step = 8
    for start in range(0, members, step):
        part = twice[start : start + step, 0:share, :].reshape(step * share, width)
        rows = halves(part)
        twice_inner = sum(
            lax.dot_general(left, right, (((1,), (1,)), ((), ())), preferred_element_type=jnp.float32)
            for left in reversed(rows)
            for right in reversed(columns)
        )
        part_sq = 0.25 * jnp.sum(part * part, axis=1, keepdims=True)
        block = (twice_inner - part_sq - train_sq) * scale
        out[start * share : (start + step) * share, :] = block
        pieces += row_logs(block, weights)
    send(pieces, logs)


def column_kernel(got, mass, col_pot, gen_mass, out):
    count, cols = got.shape[0], mass.shape[1]
    logs = [got[k, :, 0:cols] for k in range(count)]
    highest = functools.reduce(jnp.maximum, logs)
    total = weighted = jnp.zeros_like(highest)
    sums = jnp.zeros_like(gen_mass)
    for k in range(count):
        share = jnp.exp(logs[k] - highest)
        total += share
        weighted += share * got[k, :, cols : 2 * cols]
        sums += got[k, :, 2 * cols :]
    potential = -(highest + jnp.log(total))
    col_pot[...] = potential
    gen_mass[...] = sums
    costs = mass[...] * (weighted / total)
    lanes = [slice(at, at + LANES) for at in range(0, cols, LANES)]
    cost = sum(costs[:, at] for at in lanes)
    train_mass = sum(mass[:, at] for at in lanes)
    for k in range(out.shape[0]):
        out[k, :, 0:LANES] = cost
        out[k, :, LANES : 2 * LANES] = train_mass
        out[k, :, 2 * LANES :] = potential


def outputs_kernel(got, row_pot, col_pot, gen_mass, row_out, col_out, cost_out):
    terms = [got[k, :, 0 : 2 * LANES] + got[k + 1, :, 0 : 2 * LANES] for k in range(0, got.shape[0], 2)]
    sums = functools.reduce(jnp.add, terms)
    cost = jnp.sum(sums[:, 0:LANES], axis=1, keepdims=True)
    train_total = jnp.sum(sums[:, LANES:], axis=1, keepdims=True)
    columns = jnp.where(own(col_pot.shape), col_pot[...], got[partner(), :, 2 * LANES :])
    log_train = jnp.log(train_total)
    log_gen = jnp.log(jnp.sum(gen_mass[...], axis=1, keepdims=True))
    row_out[...] = EPSILON * (row_pot[...] + (ITERS * log_train - (ITERS - 1) * log_gen))
    col_out[...] = EPSILON * (columns + ITERS * (log_gen - log_train))
    cost_out[...] = -EPSILON * cost / train_total


def shards(n_gen, n_train, gen_embed, train_embed, row_mass, col_mass):
    width = gen_embed.shape[1]
    rows, cols = row_mass.shape[0], col_mass.shape[0]
    both = ("gen", "train")
    groups = [
        [g * n_train + first + (g + shift) % 2 for g in range(n_gen)]
        for first in range(0, n_train, 2)
        for shift in range(2)
    ]
    small = 1 << 20
    height = gen_embed.shape[0] + 8
    many = 8
    (packed,) = call(
        copies_kernel,
        [shape(n_train, height, width)],
        [gen_embed, col_mass[None]],
        scratch=[
            pltpu.VMEM(gen_embed.shape, jnp.float32),
            pltpu.VMEM((1, cols), jnp.float32),
            pltpu.VMEM((many, height, width), jnp.float32),
            pltpu.SemaphoreType.DMA((2,)),
            pltpu.SemaphoreType.DMA((n_train // many,)),
        ],
        in_specs=[ANY, ANY],
        out_specs=[ANY],
        limit=60 << 20,
    )
    twice = 2.0 * lax.all_to_all(packed, "train", 0, 0)
    train_block = lax.all_gather(train_embed, both, axis=0, tiled=True, axis_index_groups=groups)
    affinity, tile_mass, log_train, packed = call(
        functools.partial(affinity_kernel, 1.0 / (width * EPSILON)),
        [shape(rows, cols), shape(1, cols), shape(1, cols), shape(n_train, 1, rows)],
        [twice, train_block],
    )

    for iteration in range(ITERS):
        last = iteration == ITERS - 1
        got = lax.all_to_all(packed, "train", 0, 0)
        *row_pot, packed = call(
            functools.partial(gen_kernel, last),
            [shape(1, rows), shape(n_gen, 1, 2 * cols + LANES)] if last else [shape(n_gen, 1, cols)],
            [got, row_mass[None], affinity],
            scratch=[pltpu.VMEM((rows, LANES), jnp.float32)],
        )
        got = lax.all_to_all(packed, both, 0, 0, axis_index_groups=groups)
        if not last:
            (packed,) = call(train_kernel, [shape(n_train, 1, rows)], [got, log_train, affinity])
    col_pot, gen_mass, packed = call(
        column_kernel,
        [shape(1, cols), shape(1, LANES), shape(n_train, 1, 2 * LANES + cols)],
        [got, tile_mass],
        limit=small,
    )
    got = lax.all_to_all(packed, "train", 0, 0)
    row_out, col_out, cost = call(
        outputs_kernel,
        [shape(1, rows), shape(1, cols), shape(1, 1)],
        [got, *row_pot, col_pot, gen_mass],
        limit=small,
    )
    return (row_out.reshape(rows), col_out.reshape(cols), cost.reshape(()))


def solution(mesh):
    in_specs = (P(("gen", "train"), None), P(("train", "gen"), None), P("gen"), P("train"))
    out_specs = (P("gen"), P("train"), P())

    def body(*args):
        return shards(mesh.shape["gen"], mesh.shape["train"], *args)

    return jax.shard_map(body, mesh=mesh, in_specs=in_specs, out_specs=out_specs, check_vma=False)
```

```python
import functools
import math

import jax
import jax.numpy as jnp
from jax import lax
from jax.experimental import pallas as pl
from jax.experimental.pallas import tpu as pltpu
from jax.sharding import PartitionSpec as P

ITERS = 3


EPSILON = 0.05
UNIT = EPSILON * math.log(2.0)
LANES = 128
VMEM = pl.BlockSpec(memory_space=pltpu.VMEM)
ANY = pl.BlockSpec(memory_space=pl.ANY)


def shape(*dims):
    return jax.ShapeDtypeStruct(dims, jnp.float32)


def call(kernel, outs, ins, scratch=(), in_specs=None, out_specs=None, limit=8 << 20):
    return pl.pallas_call(
        kernel,
        out_shape=outs,
        in_specs=in_specs or [VMEM] * len(ins),
        out_specs=out_specs or [VMEM] * len(outs),
        scratch_shapes=scratch,
        compiler_params=pltpu.CompilerParams(vmem_limit_bytes=limit),
    )(*ins)


def own(shape):
    column = lax.broadcasted_iota(jnp.int32, shape, len(shape) - 1)
    share = shape[-1] // lax.axis_size("gen")
    return (column // share) % 2 == lax.axis_index("gen") % 2


def partner():
    at = lax.axis_index("train")
    return at + 1 - 2 * (at % 2)


def copies_kernel(values, mass, out, rows, row_mass, block, in_sems, sems):
    many, height, width = block.shape
    share, cols = rows.shape[0], row_mass.shape[1]
    fetches = [
        pltpu.make_async_copy(values, rows, in_sems.at[0]),
        pltpu.make_async_copy(mass, row_mass, in_sems.at[1]),
    ]
    for fetch in fetches:
        fetch.start()
    for fetch in fetches:
        fetch.wait()
    masses = jnp.concatenate([row_mass[:, at : at + width] for at in range(0, cols, width)], axis=0)
    rest = jnp.zeros((height - share - cols // width, width), jnp.float32)
    whole = jnp.concatenate([rows[...], masses, rest], axis=0)
    for k in range(many):
        block[k] = whole
    moves = [
        pltpu.make_async_copy(block, out.at[pl.ds(k * many, many)], sems.at[k]) for k in range(out.shape[0] // many)
    ]
    for move in moves:
        move.start()
    for move in moves:
        move.wait()


def halves(values):
    high = values.astype(jnp.bfloat16)
    return high, (values - high.astype(jnp.float32)).astype(jnp.bfloat16)


def combined(got, cols):
    logs = [got[k, :, 0:cols] for k in range(got.shape[0])]
    highest = functools.reduce(jnp.maximum, logs)
    return highest + jnp.log2(sum(jnp.exp2(log - highest) for log in logs))


def row_logs(block, weights):
    starts = range(0, block.shape[0], LANES)

    def scores(at):
        return block[at : at + LANES, :] + weights

    highest = [jnp.max(scores(at), axis=1, keepdims=True) for at in starts]
    totals = [jnp.sum(jnp.exp2(scores(at) - high), axis=1, keepdims=True) for at, high in zip(starts, highest)]
    logs = [high + jnp.log2(total) for high, total in zip(highest, totals)]
    return [jnp.broadcast_to(log, (LANES, LANES)).T[0:1, :] for log in logs]


def send(pieces, out):
    whole = jnp.concatenate(pieces, axis=1)
    for k in range(out.shape[0]):
        out[k] = whole


def train_kernel(got, log_train, affinity, out):
    send(row_logs(affinity, log_train[...] - combined(got, log_train.shape[1])), out)


def gen_kernel(last, got, mass, affinity, *outs):
    rows, cols = affinity.shape
    out, offsets = outs[-2:]
    potential = -combined(got, rows)
    if last:
        outs[0][...] = potential
    weights = potential + jnp.log2(mass[...])
    lanes = cols // LANES
    sub = 8

    def fold(reduce, block):
        return reduce(block.reshape(LANES // sub, sub, cols), axis=0)

    def scores(at):
        return affinity[at : at + LANES, :] + jnp.concatenate([offsets[at : at + LANES, :]] * lanes, axis=1)

    highest = None
    for at in range(0, rows, LANES):
        offsets[at : at + LANES, :] = jnp.broadcast_to(weights[:, at : at + LANES], (LANES, LANES)).T
        part = fold(jnp.max, scores(at))
        highest = part if highest is None else jnp.maximum(highest, part)
    highest = jnp.max(highest, axis=0, keepdims=True)
    total = mean = jnp.zeros((sub, cols), jnp.float32)
    for at in range(0, rows, LANES):
        share = jnp.exp2(scores(at) - highest)
        total += fold(jnp.sum, share)
        if last:
            mean += fold(jnp.sum, share * affinity[at : at + LANES, :])
    total = jnp.sum(total, axis=0, keepdims=True)
    logs = highest + jnp.log2(total)
    if last:
        mean = jnp.sum(mean, axis=0, keepdims=True) / total
        masses = sum(mass[:, at : at + LANES] for at in range(0, rows, LANES))
        send([logs, mean, masses], out)
    else:
        send([logs], out)


def affinity_kernel(scale, twice, train, out, tile_mass, log_mass, logs):
    members, _, width = twice.shape
    share = out.shape[0] // members
    cols = out.shape[1]

    def mass_of(member):
        held = twice[member, share : share + cols // width, :]
        return 0.5 * jnp.concatenate([held[k : k + 1] for k in range(cols // width)], axis=1)

    masses = jnp.where(own((1, cols)), mass_of(lax.axis_index("train")), mass_of(partner()))
    tile_mass[...] = masses
    weights = jnp.log2(masses)
    log_mass[...] = weights
    columns = halves(train[...])
    squares = [train[at : at + LANES, :] * train[at : at + LANES, :] for at in range(0, cols, LANES)]
    squares = [jnp.sum(part, axis=1, keepdims=True) for part in squares]
    train_sq = jnp.concatenate([jnp.broadcast_to(part, (LANES, LANES)).T[0:1, :] for part in squares], axis=1)
    pieces = []
    step = 8
    for start in range(0, members, step):
        part = twice[start : start + step, 0:share, :].reshape(step * share, width)
        rows = halves(part)
        twice_inner = sum(
            lax.dot_general(left, right, (((1,), (1,)), ((), ())), preferred_element_type=jnp.float32)
            for left in reversed(rows)
            for right in reversed(columns)
        )
        part_sq = 0.25 * jnp.sum(part * part, axis=1, keepdims=True)
        block = (twice_inner - part_sq - train_sq) * scale
        out[start * share : (start + step) * share, :] = block
        pieces += row_logs(block, weights)
    send(pieces, logs)


def column_kernel(got, mass, col_pot, gen_mass, out):
    count, cols = got.shape[0], mass.shape[1]
    logs = [got[k, :, 0:cols] for k in range(count)]
    highest = functools.reduce(jnp.maximum, logs)
    total = weighted = jnp.zeros_like(highest)
    sums = jnp.zeros_like(gen_mass)
    for k in range(count):
        share = jnp.exp2(logs[k] - highest)
        total += share
        weighted += share * got[k, :, cols : 2 * cols]
        sums += got[k, :, 2 * cols :]
    potential = -(highest + jnp.log2(total))
    col_pot[...] = potential
    gen_mass[...] = sums
    costs = mass[...] * (weighted / total)
    lanes = [slice(at, at + LANES) for at in range(0, cols, LANES)]
    cost = sum(costs[:, at] for at in lanes)
    train_mass = sum(mass[:, at] for at in lanes)
    for k in range(out.shape[0]):
        out[k, :, 0:LANES] = cost
        out[k, :, LANES : 2 * LANES] = train_mass
        out[k, :, 2 * LANES :] = potential


def outputs_kernel(got, row_pot, col_pot, gen_mass, row_out, col_out, cost_out):
    terms = [got[k, :, 0 : 2 * LANES] + got[k + 1, :, 0 : 2 * LANES] for k in range(0, got.shape[0], 2)]
    sums = functools.reduce(jnp.add, terms)
    cost = jnp.sum(sums[:, 0:LANES], axis=1, keepdims=True)
    train_total = jnp.sum(sums[:, LANES:], axis=1, keepdims=True)
    columns = jnp.where(own(col_pot.shape), col_pot[...], got[partner(), :, 2 * LANES :])
    log_train = jnp.log2(train_total)
    log_gen = jnp.log2(jnp.sum(gen_mass[...], axis=1, keepdims=True))
    row_out[...] = UNIT * (row_pot[...] + (ITERS * log_train - (ITERS - 1) * log_gen))
    col_out[...] = UNIT * (columns + ITERS * (log_gen - log_train))
    cost_out[...] = -UNIT * cost / train_total


def shards(n_gen, n_train, gen_embed, train_embed, row_mass, col_mass):
    width = gen_embed.shape[1]
    rows, cols = row_mass.shape[0], col_mass.shape[0]
    both = ("gen", "train")
    groups = [
        [g * n_train + first + (g + shift) % 2 for g in range(n_gen)]
        for first in range(0, n_train, 2)
        for shift in range(2)
    ]
    small = 1 << 20
    height = gen_embed.shape[0] + 8
    many = 8
    (packed,) = call(
        copies_kernel,
        [shape(n_train, height, width)],
        [gen_embed, col_mass[None]],
        scratch=[
            pltpu.VMEM(gen_embed.shape, jnp.float32),
            pltpu.VMEM((1, cols), jnp.float32),
            pltpu.VMEM((many, height, width), jnp.float32),
            pltpu.SemaphoreType.DMA((2,)),
            pltpu.SemaphoreType.DMA((n_train // many,)),
        ],
        in_specs=[ANY, ANY],
        out_specs=[ANY],
        limit=60 << 20,
    )
    twice = 2.0 * lax.all_to_all(packed, "train", 0, 0)
    train_block = lax.all_gather(train_embed, both, axis=0, tiled=True, axis_index_groups=groups)
    affinity, tile_mass, log_train, packed = call(
        functools.partial(affinity_kernel, 1.0 / (width * UNIT)),
        [shape(rows, cols), shape(1, cols), shape(1, cols), shape(n_train, 1, rows)],
        [twice, train_block],
    )

    for iteration in range(ITERS):
        last = iteration == ITERS - 1
        got = lax.all_to_all(packed, "train", 0, 0)
        *row_pot, packed = call(
            functools.partial(gen_kernel, last),
            [shape(1, rows), shape(n_gen, 1, 2 * cols + LANES)] if last else [shape(n_gen, 1, cols)],
            [got, row_mass[None], affinity],
            scratch=[pltpu.VMEM((rows, LANES), jnp.float32)],
        )
        got = lax.all_to_all(packed, both, 0, 0, axis_index_groups=groups)
        if not last:
            (packed,) = call(train_kernel, [shape(n_train, 1, rows)], [got, log_train, affinity])
    col_pot, gen_mass, packed = call(
        column_kernel,
        [shape(1, cols), shape(1, LANES), shape(n_train, 1, 2 * LANES + cols)],
        [got, tile_mass],
        limit=small,
    )
    got = lax.all_to_all(packed, "train", 0, 0)
    row_out, col_out, cost = call(
        outputs_kernel,
        [shape(1, rows), shape(1, cols), shape(1, 1)],
        [got, *row_pot, col_pot, gen_mass],
        limit=small,
    )
    return (row_out.reshape(rows), col_out.reshape(cols), cost.reshape(()))


def solution(mesh):
    in_specs = (P(("gen", "train"), None), P(("train", "gen"), None), P("gen"), P("train"))
    out_specs = (P("gen"), P("train"), P())

    def body(*args):
        return shards(mesh.shape["gen"], mesh.shape["train"], *args)

    return jax.shard_map(body, mesh=mesh, in_specs=in_specs, out_specs=out_specs, check_vma=False)
```

```python
import functools
import math

import jax
import jax.numpy as jnp
from jax import lax
from jax.experimental import pallas as pl
from jax.experimental.pallas import tpu as pltpu
from jax.sharding import PartitionSpec as P

ITERS = 3


EPSILON = 0.05
UNIT = EPSILON * math.log(2.0)
LANES = 128
VMEM = pl.BlockSpec(memory_space=pltpu.VMEM)
ANY = pl.BlockSpec(memory_space=pl.ANY)


def shape(*dims):
    return jax.ShapeDtypeStruct(dims, jnp.float32)


def call(kernel, outs, ins, scratch=(), in_specs=None, out_specs=None, limit=8 << 20):
    return pl.pallas_call(
        kernel,
        out_shape=outs,
        in_specs=in_specs or [VMEM] * len(ins),
        out_specs=out_specs or [VMEM] * len(outs),
        scratch_shapes=scratch,
        compiler_params=pltpu.CompilerParams(vmem_limit_bytes=limit),
    )(*ins)


def own(shape):
    column = lax.broadcasted_iota(jnp.int32, shape, len(shape) - 1)
    share = shape[-1] // lax.axis_size("gen")
    return (column // share) % 2 == lax.axis_index("gen") % 2


def partner():
    at = lax.axis_index("train")
    return at + 1 - 2 * (at % 2)


def copies_kernel(values, mass, out, rows, row_mass, block, in_sems, sems):
    many, height, width = block.shape
    share, cols = rows.shape[0], row_mass.shape[1]
    fetches = [
        pltpu.make_async_copy(values, rows, in_sems.at[0]),
        pltpu.make_async_copy(mass, row_mass, in_sems.at[1]),
    ]
    for fetch in fetches:
        fetch.start()
    for fetch in fetches:
        fetch.wait()
    masses = jnp.concatenate([row_mass[:, at : at + width] for at in range(0, cols, width)], axis=0)
    rest = jnp.zeros((height - share - cols // width, width), jnp.float32)
    whole = jnp.concatenate([rows[...], masses, rest], axis=0)
    for k in range(many):
        block[k] = whole
    moves = [
        pltpu.make_async_copy(block, out.at[pl.ds(k * many, many)], sems.at[k]) for k in range(out.shape[0] // many)
    ]
    for move in moves:
        move.start()
    for move in moves:
        move.wait()


def halves(values):
    high = values.astype(jnp.bfloat16)
    return high, (values - high.astype(jnp.float32)).astype(jnp.bfloat16)


def combined(got, cols):
    logs = [got[k, :, 0:cols] for k in range(got.shape[0])]
    highest = functools.reduce(jnp.maximum, logs)
    return highest + jnp.log2(sum(jnp.exp2(log - highest) for log in logs))


def row_logs(block, weights):
    starts = range(0, block.shape[0], LANES)

    def scores(at):
        return block[at : at + LANES, :] + weights

    highest = [jnp.max(scores(at), axis=1, keepdims=True) for at in starts]
    totals = [jnp.sum(jnp.exp2(scores(at) - high), axis=1, keepdims=True) for at, high in zip(starts, highest)]
    logs = [high + jnp.log2(total) for high, total in zip(highest, totals)]
    return [jnp.broadcast_to(log, (LANES, LANES)).T[0:1, :] for log in logs]


def send(pieces, out):
    whole = jnp.concatenate(pieces, axis=1)
    for k in range(out.shape[0]):
        out[k] = whole


def train_kernel(got, log_train, affinity, out):
    send(row_logs(affinity, log_train[...] - combined(got, log_train.shape[1])), out)


def gen_kernel(last, got, mass, affinity, *outs):
    rows, cols = affinity.shape
    out, held = outs[-2:]
    potential = -combined(got, rows)
    if last:
        outs[0][...] = potential
    weights = potential + jnp.log2(mass[...])
    lanes = cols // LANES
    sub = 8

    def fold(reduce, block):
        return reduce(block.reshape(LANES // sub, sub, cols), axis=0)

    highest = None
    for at in range(0, rows, LANES):
        offsets = jnp.broadcast_to(weights[:, at : at + LANES], (LANES, LANES)).T
        scores = affinity[at : at + LANES, :] + jnp.concatenate([offsets] * lanes, axis=1)
        held[at : at + LANES, :] = scores
        part = fold(jnp.max, scores)
        highest = part if highest is None else jnp.maximum(highest, part)
    highest = jnp.max(highest, axis=0, keepdims=True)
    total = mean = jnp.zeros((sub, cols), jnp.float32)
    for at in range(0, rows, LANES):
        share = jnp.exp2(held[at : at + LANES, :] - highest)
        total += fold(jnp.sum, share)
        if last:
            mean += fold(jnp.sum, share * affinity[at : at + LANES, :])
    total = jnp.sum(total, axis=0, keepdims=True)
    logs = highest + jnp.log2(total)
    if last:
        mean = jnp.sum(mean, axis=0, keepdims=True) / total
        masses = sum(mass[:, at : at + LANES] for at in range(0, rows, LANES))
        send([logs, mean, masses], out)
    else:
        send([logs], out)


def affinity_kernel(scale, twice, train, out, tile_mass, log_mass, logs):
    members, _, width = twice.shape
    share = out.shape[0] // members
    cols = out.shape[1]

    def mass_of(member):
        held = twice[member, share : share + cols // width, :]
        return 0.5 * jnp.concatenate([held[k : k + 1] for k in range(cols // width)], axis=1)

    masses = jnp.where(own((1, cols)), mass_of(lax.axis_index("train")), mass_of(partner()))
    tile_mass[...] = masses
    weights = jnp.log2(masses)
    log_mass[...] = weights
    columns = halves(train[...])
    squares = [train[at : at + LANES, :] * train[at : at + LANES, :] for at in range(0, cols, LANES)]
    squares = [jnp.sum(part, axis=1, keepdims=True) for part in squares]
    train_sq = jnp.concatenate([jnp.broadcast_to(part, (LANES, LANES)).T[0:1, :] for part in squares], axis=1)
    pieces = []
    step = 8
    for start in range(0, members, step):
        part = twice[start : start + step, 0:share, :].reshape(step * share, width)
        rows = halves(part)
        twice_inner = sum(
            lax.dot_general(left, right, (((1,), (1,)), ((), ())), preferred_element_type=jnp.float32)
            for left in reversed(rows)
            for right in reversed(columns)
        )
        part_sq = 0.25 * jnp.sum(part * part, axis=1, keepdims=True)
        block = (twice_inner - part_sq - train_sq) * scale
        out[start * share : (start + step) * share, :] = block
        pieces += row_logs(block, weights)
    send(pieces, logs)


def column_kernel(got, mass, col_pot, gen_mass, out):
    count, cols = got.shape[0], mass.shape[1]
    logs = [got[k, :, 0:cols] for k in range(count)]
    highest = functools.reduce(jnp.maximum, logs)
    total = weighted = jnp.zeros_like(highest)
    sums = jnp.zeros_like(gen_mass)
    for k in range(count):
        share = jnp.exp2(logs[k] - highest)
        total += share
        weighted += share * got[k, :, cols : 2 * cols]
        sums += got[k, :, 2 * cols :]
    potential = -(highest + jnp.log2(total))
    col_pot[...] = potential
    gen_mass[...] = sums
    costs = mass[...] * (weighted / total)
    lanes = [slice(at, at + LANES) for at in range(0, cols, LANES)]
    cost = sum(costs[:, at] for at in lanes)
    train_mass = sum(mass[:, at] for at in lanes)
    for k in range(out.shape[0]):
        out[k, :, 0:LANES] = cost
        out[k, :, LANES : 2 * LANES] = train_mass
        out[k, :, 2 * LANES :] = potential


def outputs_kernel(got, row_pot, col_pot, gen_mass, row_out, col_out, cost_out):
    terms = [got[k, :, 0 : 2 * LANES] + got[k + 1, :, 0 : 2 * LANES] for k in range(0, got.shape[0], 2)]
    sums = functools.reduce(jnp.add, terms)
    cost = jnp.sum(sums[:, 0:LANES], axis=1, keepdims=True)
    train_total = jnp.sum(sums[:, LANES:], axis=1, keepdims=True)
    columns = jnp.where(own(col_pot.shape), col_pot[...], got[partner(), :, 2 * LANES :])
    log_train = jnp.log2(train_total)
    log_gen = jnp.log2(jnp.sum(gen_mass[...], axis=1, keepdims=True))
    row_out[...] = UNIT * (row_pot[...] + (ITERS * log_train - (ITERS - 1) * log_gen))
    col_out[...] = UNIT * (columns + ITERS * (log_gen - log_train))
    cost_out[...] = -UNIT * cost / train_total


def shards(n_gen, n_train, gen_embed, train_embed, row_mass, col_mass):
    width = gen_embed.shape[1]
    rows, cols = row_mass.shape[0], col_mass.shape[0]
    both = ("gen", "train")
    groups = [
        [g * n_train + first + (g + shift) % 2 for g in range(n_gen)]
        for first in range(0, n_train, 2)
        for shift in range(2)
    ]
    small = 1 << 20
    height = gen_embed.shape[0] + 8
    many = 8
    (packed,) = call(
        copies_kernel,
        [shape(n_train, height, width)],
        [gen_embed, col_mass[None]],
        scratch=[
            pltpu.VMEM(gen_embed.shape, jnp.float32),
            pltpu.VMEM((1, cols), jnp.float32),
            pltpu.VMEM((many, height, width), jnp.float32),
            pltpu.SemaphoreType.DMA((2,)),
            pltpu.SemaphoreType.DMA((n_train // many,)),
        ],
        in_specs=[ANY, ANY],
        out_specs=[ANY],
        limit=60 << 20,
    )
    twice = 2.0 * lax.all_to_all(packed, "train", 0, 0)
    train_block = lax.all_gather(train_embed, both, axis=0, tiled=True, axis_index_groups=groups)
    affinity, tile_mass, log_train, packed = call(
        functools.partial(affinity_kernel, 1.0 / (width * UNIT)),
        [shape(rows, cols), shape(1, cols), shape(1, cols), shape(n_train, 1, rows)],
        [twice, train_block],
    )

    for iteration in range(ITERS):
        last = iteration == ITERS - 1
        got = lax.all_to_all(packed, "train", 0, 0)
        *row_pot, packed = call(
            functools.partial(gen_kernel, last),
            [shape(1, rows), shape(n_gen, 1, 2 * cols + LANES)] if last else [shape(n_gen, 1, cols)],
            [got, row_mass[None], affinity],
            scratch=[pltpu.VMEM((rows, cols), jnp.float32)],
        )
        got = lax.all_to_all(packed, both, 0, 0, axis_index_groups=groups)
        if not last:
            (packed,) = call(train_kernel, [shape(n_train, 1, rows)], [got, log_train, affinity])
    col_pot, gen_mass, packed = call(
        column_kernel,
        [shape(1, cols), shape(1, LANES), shape(n_train, 1, 2 * LANES + cols)],
        [got, tile_mass],
        limit=small,
    )
    got = lax.all_to_all(packed, "train", 0, 0)
    row_out, col_out, cost = call(
        outputs_kernel,
        [shape(1, rows), shape(1, cols), shape(1, 1)],
        [got, *row_pot, col_pot, gen_mass],
        limit=small,
    )
    return (row_out.reshape(rows), col_out.reshape(cols), cost.reshape(()))


def solution(mesh):
    in_specs = (P(("gen", "train"), None), P(("train", "gen"), None), P("gen"), P("train"))
    out_specs = (P("gen"), P("train"), P())

    def body(*args):
        return shards(mesh.shape["gen"], mesh.shape["train"], *args)

    return jax.shard_map(body, mesh=mesh, in_specs=in_specs, out_specs=out_specs, check_vma=False)
```
